32 devices in a mesh: wide: 8 (over z, y), pair: 4 (over x, core).
Axes of the slice: x: 2, y: 2, z: 4, core: 2. Of those that a mesh axis runs over, the one named last changes fastest.
Arguments:
- three_center: bfloat16 [32, 8, 1024], P('wide'), may hold values from -1.25 to 1.25
- occ_green: bfloat16 [32, 8, 8, 8], P('wide', 'pair'), may hold values from -2 to 2
- virt_green: bfloat16 [32, 8, 8, 8], P('wide', 'pair'), may hold values from -2 to 2
- occ_column: int32 [32, 8], P('wide', 'pair'), may hold values from 0 to 31, as said below
- partner_live: int32 [32, 8], P('wide', 'pair'), may hold values 0 or 1
Outputs:
- response: float32 [128, 128], P('pair')
The draws below stay inside these ranges and needn't reach their ends.
Inputs may be any that keep to these rules, and one draw needn't show every extreme that they name: `occ_column`: for each index of pair and each index w of wide, the slots of that group on the 4 atom blocks w * 4 to w * 4 + 3 name partner blocks k such that no value of k // 4 occurs more than 2 times, and some value occurs exactly 2 times.
All inputs are finite; a program needn't handle non-finite values. No bound on the sum of `partner_live` on one device may be relied on, other than what follows from the above.
Results may differ from the reference program's by a relative error of at most 0.004.
Values may be sent and summed in bfloat16 or wider, within the bound.
No kernel may reach another device: no remote copies, remote signals or barrier semaphores. Data moves between devices by JAX's collectives and lax.ppermute only.
A program may use at most 64 MiB of HBM per device.

```python
import jax
import jax.numpy as jnp
from jax import lax

BS = 8
PB = 128
AD = 4
CAP = 2
KP = 2
KO = 8
NA = 32
N_PAIR = 4


def draw_occ_column(key, part):
    owner_total = NA // AD
    group_total = KO // KP
    slot_total = owner_total * CAP
    unit_total = AD * KP
    slot_owner = jnp.repeat(jnp.arange(owner_total, dtype=jnp.int32), CAP)
    favour = jax.random.randint(jax.random.fold_in(key, 11), (owner_total,), 0, 2) * 2048

    def one_group(index):
        subkey = jax.random.fold_in(key, index + 100)
        key_list = jax.random.split(subkey, 4)
        score = jax.random.randint(key_list[0], (slot_total,), 0, 4096) + favour[slot_owner]
        forced = jax.random.randint(key_list[1], (), 0, owner_total)
        score = jnp.where(slot_owner == forced, 8192, score)
        distinct = score * slot_total + jnp.arange(slot_total, dtype=jnp.int32)
        _, chosen = lax.top_k(distinct, unit_total)
        owners = slot_owner[chosen]
        owners = owners[jax.random.permutation(key_list[2], unit_total)]
        local_row = jax.random.randint(key_list[3], (unit_total,), 0, AD)
        return owners * AD + local_row
    table = jax.vmap(one_group)(jnp.arange(owner_total * group_total, dtype=jnp.int32))
    table = table.reshape(owner_total, group_total, AD, KP).transpose(0, 2, 1, 3)
    return table.reshape(owner_total * AD, group_total * KP).astype(jnp.int32)


def with_ends(result, stream_key, least, top_value):
    extent = result.shape
    spot = [jax.random.randint(jax.random.fold_in(stream_key, axis), (), 0, extent[axis]) for axis in range(len(extent))]
    result = result.at[tuple(spot)].set(least)
    longest = extent.index(max(extent))
    spot[longest] = (spot[longest] + 1) % extent[longest]
    return result.at[tuple(spot)].set(top_value)


def levels(own_key, dims, pieces, smallest, top_value):
    def one(axis_at, shards_of):
        heights = jax.random.uniform(jax.random.fold_in(jax.random.fold_in(own_key, 6), axis_at), (shards_of,), jnp.float32, smallest / len(pieces), top_value / len(pieces))
        return jnp.repeat(jnp.exp(heights), dims[axis_at] // shards_of).reshape((-1,) + (1,) * (len(dims) - axis_at - 1))

    loudness = one(*pieces[0])
    for cut in pieces[1:]:
        loudness = loudness * one(*cut)
    return loudness


def normal_values(own_key, shape, scale, bound, shards=(), held_as=jnp.bfloat16):
    array = scale * jax.random.normal(own_key, shape, jnp.float32)
    if shards:
        array = array * levels(own_key, shape, shards, -0.22, 0.18)
    return jnp.clip(array, -bound, bound).astype(held_as)


def setup_inputs(seed: int = 0) -> dict:
    keys = jax.random.split(jax.random.key(seed), 6)
    three_center = normal_values(keys[0], (NA, BS, BS * PB), ((KO * NA * BS * BS) ** -0.25), 1.25, ((0, 8),))
    occ_green = normal_values(keys[1], (NA, KO, BS, BS), BS ** -0.5, 2.0, ((0, 8), (1, 4)))
    virt_green = normal_values(keys[2], (NA, KO, BS, BS), BS ** -0.5, 2.0, ((0, 8), (1, 4)))
    occ_column = draw_occ_column(jax.random.fold_in(keys[5], 71), 0)
    partner_live = with_ends((jax.random.randint(keys[4], (NA, KO), 0, 5) < 4).astype(jnp.int32), jax.random.fold_in(keys[4], 1), 0, 1)
    return {"three_center": three_center, "occ_green": occ_green, "virt_green": virt_green, "occ_column": occ_column, "partner_live": partner_live}


def round_trip(values):
    return lax.optimization_barrier(values.astype(jnp.bfloat16)).astype(jnp.float32)


def reference(three_center, occ_green, virt_green, occ_column, partner_live):
    atom_count = three_center.shape[0]
    blocks = three_center.astype(jnp.float32)
    flat_blocks = blocks.reshape(atom_count * BS * BS, PB)
    response = jnp.zeros((PB, PB), jnp.float32)
    for pair_group in range(N_PAIR):
        def add_slot(partner_sum, slot):
            occ_block = lax.dynamic_index_in_dim(occ_green, slot, 1, False).astype(jnp.float32)
            virt_block = lax.dynamic_index_in_dim(virt_green, slot, 1, False).astype(jnp.float32)
            target = lax.dynamic_index_in_dim(occ_column, slot, 1, False).astype(jnp.int32)
            weight = lax.dynamic_index_in_dim(partner_live, slot, 1, False).astype(jnp.float32)
            occupied_part = jnp.einsum("anl,anx->alx", occ_block, blocks, precision=lax.Precision.HIGHEST)
            occupied_part = round_trip(occupied_part * weight[:, None, None])
            both_part = jnp.einsum("alnp,ans->alsp", occupied_part.reshape(atom_count, BS, BS, PB), virt_block, precision=lax.Precision.HIGHEST)
            both_part = round_trip(both_part)
            partner_sum = partner_sum.at[target].add(both_part.reshape(atom_count, BS * BS * PB))
            return partner_sum, None

        start = jnp.zeros((atom_count, BS * BS * PB), jnp.float32)
        slot_list = jnp.arange(KP, dtype=jnp.int32) + pair_group * KP
        partner_sum, _ = lax.scan(add_slot, start, slot_list)
        summed = partner_sum.reshape(atom_count * BS * BS, PB)
        response = response + jnp.dot(summed.T, flat_blocks, precision=lax.Precision.HIGHEST, preferred_element_type=jnp.float32)
    return response
```

```python
import functools

import jax
import jax.numpy as jnp
from jax import lax
from jax.experimental import pallas as pl
from jax.experimental.pallas import tpu as pltpu
from jax.sharding import PartitionSpec as P

CHUNK = 4
BASE = 256
F32, BF16 = jnp.float32, jnp.bfloat16


def ceil_to(value, step):
    return -(-value // step) * step


def small_layout(unit_count, block_size):
    chunk_count = -(-unit_count // CHUNK)
    column_at = chunk_count * 2 * CHUNK * block_size
    return chunk_count, column_at, ceil_to(column_at + 2 * unit_count, 128)


def iota(shape, axis):
    return lax.broadcasted_iota(jnp.int32, shape, axis)


def pack_kernel(half_ref, column_ref, live_ref, tc_ref, occ_ref, virt_ref, block_ref, small_ref):
    local_atoms, own_units, block_size, _ = occ_ref.shape
    wide_row = tc_ref.shape[2]
    unit_count = 2 * own_units
    _, column_at, lanes = small_layout(unit_count, block_size)
    half = half_ref[0]
    row, lane = iota((block_size, lanes), 0), iota((block_size, lanes), 1)
    packed = jnp.zeros((local_atoms * block_size, lanes), F32)
    columns = [jnp.zeros((block_size, lanes), F32) for _ in range(local_atoms)]
    for slot in range(own_units):
        unit = half * own_units + slot
        at = (unit // CHUNK) * (2 * CHUNK * block_size) + (unit % CHUNK) * block_size
        occ = jnp.concatenate(
            [
                occ_ref[atom, slot].astype(F32) * live_ref[atom, slot].astype(F32)
                for atom in range(local_atoms)
            ],
            axis=0,
        ).astype(BF16)
        virt = jnp.concatenate(
            [virt_ref[atom, slot].astype(F32) for atom in range(local_atoms)], axis=0
        ).astype(BF16)
        occ_place = (lane == at + row).astype(BF16)
        virt_place = (lane == at + CHUNK * block_size + row).astype(BF16)
        packed += jnp.dot(occ, occ_place, preferred_element_type=F32)
        packed += jnp.dot(virt, virt_place, preferred_element_type=F32)
        for atom in range(local_atoms):
            column = column_ref[atom, slot]
            high = column // BASE
            low = column - high * BASE
            columns[atom] += jnp.where(lane == column_at + unit, high.astype(F32), 0.0)
            columns[atom] += jnp.where(
                lane == column_at + unit_count + unit, low.astype(F32), 0.0
            )
    packed = (packed + jnp.concatenate(columns, axis=0)).astype(BF16)
    packed = packed.reshape(local_atoms, block_size, lanes)
    block_ref[:, :, :wide_row] = tc_ref[...]
    block_ref[:, :, wide_row:] = packed
    small_ref[...] = packed


def response_kernel(
    wide_count, unit_count, starts_ref, place_ref, *refs
):
    block_refs = refs[: -7]
    keep_ref, send_ref, rows_ref, small_ref, index_ref, column_ref, sem = refs[-7:]
    block_size = block_refs[0].shape[1]
    square = block_size * block_size
    aux_count = rows_ref.shape[2]
    chunk_count, column_at, lanes = small_layout(unit_count, block_size)
    atom_total = rows_ref.shape[0]
    local_atoms = atom_total // wide_count
    side, half = place_ref[0], place_ref[1]

    for number, block_ref in enumerate(block_refs):
        first = starts_ref[number]

        def place_atom(atom, block_ref=block_ref, first=first):
            rows_ref[first + atom] = jnp.concatenate(
                [
                    block_ref[atom, :, at * aux_count : (at + 1) * aux_count]
                    for at in range(block_size)
                ],
                axis=0,
            )
            small_ref[first + atom] = block_ref[atom, :, block_size * aux_count :]

        if block_ref.shape[0] <= 8:
            for atom in range(block_ref.shape[0]):
                place_atom(atom)
        else:
            pl.loop(0, block_ref.shape[0])(place_atom)

    own_atoms = index_ref.shape[0]
    column_tile = column_at // 128 * 128
    column_lane = column_at - column_tile

    def atom_of(position):
        return ((position // local_atoms) * 2 + (side ^ half) % 2) * local_atoms + position % local_atoms

    def place_column(position):
        digits = small_ref[atom_of(position)][:, column_tile:].astype(F32)
        index_ref[position] = digits[0:1, :].astype(jnp.int32)

    if own_atoms <= 16:
        for position in range(own_atoms):
            place_column(position)
    else:
        pl.loop(0, own_atoms)(place_column)
    copy = pltpu.make_async_copy(index_ref, column_ref, sem)
    copy.start()

    wide_unit = CHUNK * square
    spread_row, spread_lane = iota((128, 2 * wide_unit), 0), iota((128, 2 * wide_unit), 1)
    is_virt = spread_lane >= wide_unit
    inner = spread_lane % wide_unit
    unit_of, upper, lower = inner // square, (inner // block_size) % block_size, inner % block_size
    wanted = unit_of * block_size + jnp.where(is_virt, upper + CHUNK * block_size, lower)
    lane_row, lane = iota((block_size, wide_unit), 0), iota((block_size, wide_unit), 1)
    lane_unit, lane_upper, lane_lower = lane // square, (lane // block_size) % block_size, lane % block_size
    occ_mask = [(lane_upper == at).astype(F32) for at in range(block_size)]
    virt_mask = [
        ((lane_unit == at) & (lane_lower == lane_row)).astype(F32) for at in range(CHUNK)
    ]
    group = max(1, min(own_atoms, 16 // chunk_count))
    copy.wait()

    def work(step, total):
        for chunk in range(chunk_count):
            at = chunk * 2 * CHUNK * block_size
            tile = at // 128 * 128
            spread = (spread_row == wanted + (at - tile)).astype(BF16)
            atoms = [atom_of(step * group + member) for member in range(group)]
            smalls = jnp.concatenate(
                [small_ref[atom][:, tile : tile + 128] for atom in atoms], axis=0
            )
            wide = jnp.dot(smalls, spread, preferred_element_type=F32)
            for member in range(group):
                values = wide[member * block_size : (member + 1) * block_size]
                occ, virt = values[:, :wide_unit], values[:, wide_unit:]
                occ_weights = jnp.concatenate([occ * mask for mask in occ_mask], axis=0)
                virt_weights = jnp.concatenate(
                    [
                        jnp.broadcast_to(virt[nu : nu + 1], virt.shape) * virt_mask[unit]
                        for unit in range(CHUNK)
                        for nu in range(block_size)
                    ],
                    axis=0,
                )
                occupied = lax.dot_general(
                    rows_ref[atoms[member]],
                    occ_weights.astype(BF16),
                    (((0,), (0,)), ((), ())),
                    preferred_element_type=F32,
                ).astype(BF16)
                both = jnp.dot(
                    occupied, virt_weights.astype(BF16), preferred_element_type=F32
                ).astype(BF16)
                partner = []
                for unit in range(chunk * CHUNK, (chunk + 1) * CHUNK):
                    if unit < unit_count:
                        high = column_ref[step * group + member, 0, column_lane + unit]
                        low = column_ref[
                            step * group + member, 0, column_lane + unit_count + unit
                        ]
                        partner.append(rows_ref[high * BASE + low])
                    else:
                        partner.append(jnp.zeros((square, aux_count), BF16))
                total += jnp.dot(
                    both, jnp.concatenate(partner, axis=0), preferred_element_type=F32
                )
        return total

    steps = own_atoms // group
    total = jnp.zeros((aux_count, aux_count), F32)
    if steps == 1:
        total = work(0, total)
    else:
        total = lax.fori_loop(0, steps, work, total)
    row_count = keep_ref.shape[1]
    parts = [total[at * row_count : (at + 1) * row_count] for at in range(4)]
    keep = [jnp.where(half == 0, parts[2 * at], parts[2 * at + 1]) for at in range(2)]
    send = [jnp.where(half == 0, parts[2 * at + 1], parts[2 * at]) for at in range(2)]
    outer = place_ref[2]
    keep_ref[0] = jnp.where(outer == 0, keep[0], keep[1])
    keep_ref[1] = jnp.where(outer == 0, keep[1], keep[0])
    send_ref[0] = jnp.where(outer == 0, send[0], send[1])
    send_ref[1] = jnp.where(outer == 0, send[1], send[0])


VMEM = pl.BlockSpec(memory_space=pltpu.VMEM)
SMEM = pl.BlockSpec(memory_space=pltpu.SMEM)


def gather_over_wide(block, wide_count, pair_count):
    here = lax.axis_index("wide")
    if wide_count != 8:
        return [lax.all_gather(block, "wide", axis=0, tiled=True)], [jnp.int32(0)]
    half = lax.axis_index("pair") % 2
    partner = [(p, p ^ 1) for p in range(pair_count)]
    blocks, owners = [], []
    for even, odd in ((4, 5), (6, 7), (2, 3), (0, 1)):
        route = [
            ((w ^ d) * pair_count + p, w * pair_count + p)
            for w in range(wide_count)
            for p in range(pair_count)
            for d in (odd if p % 2 else even,)
            if d
        ]
        fetched = lax.ppermute(block, ("wide", "pair"), route)
        blocks += [fetched, lax.ppermute(fetched, "pair", partner)]
        owners += [here ^ jnp.where(half == 0, even, odd), here ^ jnp.where(half == 0, odd, even)]
    return blocks + [block], owners + [here]


def local(three_center, occ_green, virt_green, occ_column, partner_live):
    local_atoms, block_size, wide_row = three_center.shape
    own_units = occ_green.shape[1]
    aux_count = wide_row // block_size
    wide_count, pair_count = lax.axis_size("wide"), lax.axis_size("pair")
    unit_count = 2 * own_units
    _, column_at, lanes = small_layout(unit_count, block_size)
    pair_at = lax.axis_index("pair")
    half = pair_at % 2
    partner = [(p, p ^ 1) for p in range(pair_count)]

    block, small = pl.pallas_call(
        pack_kernel,
        out_shape=(
            jax.ShapeDtypeStruct((local_atoms, block_size, wide_row + lanes), BF16),
            jax.ShapeDtypeStruct((local_atoms, block_size, lanes), BF16),
        ),
        in_specs=[SMEM, SMEM, SMEM, VMEM, VMEM, VMEM],
        out_specs=(VMEM, VMEM),
        name="pack",
    )(half.reshape(1), occ_column, partner_live, three_center, occ_green, virt_green)
    merged = small + lax.ppermute(small, "pair", partner)
    block = lax.dynamic_update_slice(block, merged, (0, 0, wide_row))
    blocks, owners = gather_over_wide(block, wide_count, pair_count)
    starts = jnp.stack([owner * local_atoms for owner in owners]).astype(jnp.int32)
    place = jnp.stack([lax.axis_index("wide"), half, pair_at // 2]).astype(jnp.int32)

    atom_total = wide_count * local_atoms
    own_atoms = atom_total // 2
    index_lanes = lanes - column_at // 128 * 128
    row_count = aux_count // pair_count
    part = jax.ShapeDtypeStruct((2, row_count, aux_count), F32)
    keep, send = pl.pallas_call(
        functools.partial(response_kernel, wide_count, unit_count),
        out_shape=(part, part),
        in_specs=[SMEM, SMEM] + [VMEM] * len(blocks),
        out_specs=(VMEM, VMEM),
        scratch_shapes=[
            pltpu.VMEM((atom_total, block_size * block_size, aux_count), BF16),
            pltpu.VMEM((atom_total, block_size, lanes), BF16),
            pltpu.VMEM((own_atoms, 1, index_lanes), jnp.int32),
            pltpu.SMEM((own_atoms, 1, index_lanes), jnp.int32),
            pltpu.SemaphoreType.DMA,
        ],
        compiler_params=pltpu.CompilerParams(vmem_limit_bytes=56 * 2**20),
        name="response",
    )(starts, place, *blocks)
    summed = keep + lax.ppermute(send, "pair", partner)
    other = [(p, p ^ 2) for p in range(pair_count)]
    return summed[0] + lax.ppermute(summed[1], "pair", other)


def solution(mesh):
    placed = (
        P("wide", None, None),
        P("wide", "pair", None, None),
        P("wide", "pair", None, None),
        P("wide", "pair"),
        P("wide", "pair"),
    )
    return jax.shard_map(
        local, mesh=mesh, in_specs=placed, out_specs=P("pair", None), check_vma=False
    )
```

```python
import functools

import jax
import jax.numpy as jnp
from jax import lax
from jax.experimental import pallas as pl
from jax.experimental.pallas import tpu as pltpu
from jax.sharding import PartitionSpec as P

CHUNK = 4
BASE = 256
F32, BF16 = jnp.float32, jnp.bfloat16


def ceil_to(value, step):
    return -(-value // step) * step


def small_layout(unit_count, block_size):
    chunk_count = -(-unit_count // CHUNK)
    column_at = chunk_count * 2 * CHUNK * block_size
    return chunk_count, column_at, ceil_to(column_at + 2 * unit_count, 128)


def iota(shape, axis):
    return lax.broadcasted_iota(jnp.int32, shape, axis)


def pack_kernel(pair_ref, column_ref, live_ref, tc_ref, occ_ref, virt_ref, block_ref, small_ref):
    local_atoms, own_units, block_size, _ = occ_ref.shape
    wide_row = tc_ref.shape[2]
    unit_count = 2 * own_units
    _, column_at, lanes = small_layout(unit_count, block_size)
    half = pair_ref[0] % 2
    row, lane = iota((block_size, lanes), 0), iota((block_size, lanes), 1)
    packed = jnp.zeros((local_atoms * block_size, lanes), F32)
    columns = [jnp.zeros((block_size, lanes), F32) for _ in range(local_atoms)]
    for slot in range(own_units):
        unit = half * own_units + slot
        at = (unit // CHUNK) * (2 * CHUNK * block_size) + (unit % CHUNK) * block_size
        occ = jnp.concatenate(
            [
                occ_ref[atom, slot].astype(F32) * live_ref[slot, atom].astype(F32)
                for atom in range(local_atoms)
            ],
            axis=0,
        ).astype(BF16)
        virt = jnp.concatenate(
            [virt_ref[atom, slot].astype(F32) for atom in range(local_atoms)], axis=0
        ).astype(BF16)
        occ_place = (lane == at + row).astype(BF16)
        virt_place = (lane == at + CHUNK * block_size + row).astype(BF16)
        packed += jnp.dot(occ, occ_place, preferred_element_type=F32)
        packed += jnp.dot(virt, virt_place, preferred_element_type=F32)
        for atom in range(local_atoms):
            column = column_ref[slot, atom]
            high = column // BASE
            low = column - high * BASE
            columns[atom] += jnp.where(lane == column_at + unit, high.astype(F32), 0.0)
            columns[atom] += jnp.where(
                lane == column_at + unit_count + unit, low.astype(F32), 0.0
            )
    packed = (packed + jnp.concatenate(columns, axis=0)).astype(BF16)
    packed = packed.reshape(local_atoms, block_size, lanes)
    block_ref[:, :, :wide_row] = tc_ref[...]
    block_ref[:, :, wide_row:] = packed
    small_ref[...] = packed


def response_kernel(wide_count, unit_count, offsets, wide_ref, pair_ref, *refs):
    block_refs = refs[: -7]
    keep_ref, send_ref, rows_ref, small_ref, index_ref, column_ref, sem = refs[-7:]
    block_size = block_refs[0].shape[1]
    square = block_size * block_size
    aux_count = rows_ref.shape[2]
    chunk_count, column_at, lanes = small_layout(unit_count, block_size)
    atom_total = rows_ref.shape[0]
    local_atoms = atom_total // wide_count
    side, half, outer = wide_ref[0], pair_ref[0] % 2, pair_ref[0] // 2

    for number, block_ref in enumerate(block_refs):
        first = 0
        if offsets[number] is not None:
            even, odd = offsets[number]
            first = (side ^ jnp.where(half == 0, even, odd)) * local_atoms

        def place_atom(atom, block_ref=block_ref, first=first):
            rows_ref[first + atom] = jnp.concatenate(
                [
                    block_ref[atom, :, at * aux_count : (at + 1) * aux_count]
                    for at in range(block_size)
                ],
                axis=0,
            )
            small_ref[first + atom] = block_ref[atom, :, block_size * aux_count :]

        if block_ref.shape[0] <= 8:
            for atom in range(block_ref.shape[0]):
                place_atom(atom)
        else:
            pl.loop(0, block_ref.shape[0])(place_atom)

    own_atoms = index_ref.shape[0]
    column_tile = column_at // 128 * 128
    column_lane = column_at - column_tile

    def atom_of(position):
        return ((position // local_atoms) * 2 + (side ^ half) % 2) * local_atoms + position % local_atoms

    def place_column(position):
        digits = small_ref[atom_of(position)][:, column_tile:].astype(F32)
        index_ref[position] = digits[0:1, :].astype(jnp.int32)

    if own_atoms <= 16:
        for position in range(own_atoms):
            place_column(position)
    else:
        pl.loop(0, own_atoms)(place_column)
    copy = pltpu.make_async_copy(index_ref, column_ref, sem)
    copy.start()

    wide_unit = CHUNK * square
    spread_row, spread_lane = iota((128, 2 * wide_unit), 0), iota((128, 2 * wide_unit), 1)
    is_virt = spread_lane >= wide_unit
    inner = spread_lane % wide_unit
    unit_of, upper, lower = inner // square, (inner // block_size) % block_size, inner % block_size
    wanted = unit_of * block_size + jnp.where(is_virt, upper + CHUNK * block_size, lower)
    lane_row, lane = iota((block_size, wide_unit), 0), iota((block_size, wide_unit), 1)
    lane_unit, lane_upper, lane_lower = lane // square, (lane // block_size) % block_size, lane % block_size
    occ_mask = [(lane_upper == at).astype(F32) for at in range(block_size)]
    virt_mask = [
        ((lane_unit == at) & (lane_lower == lane_row)).astype(F32) for at in range(CHUNK)
    ]
    group = max(1, min(own_atoms, 16 // chunk_count))
    copy.wait()

    def work(step, total):
        for chunk in range(chunk_count):
            at = chunk * 2 * CHUNK * block_size
            tile = at // 128 * 128
            spread = (spread_row == wanted + (at - tile)).astype(BF16)
            atoms = [atom_of(step * group + member) for member in range(group)]
            smalls = jnp.concatenate(
                [small_ref[atom][:, tile : tile + 128] for atom in atoms], axis=0
            )
            wide = jnp.dot(smalls, spread, preferred_element_type=F32)
            for member in range(group):
                values = wide[member * block_size : (member + 1) * block_size]
                occ, virt = values[:, :wide_unit], values[:, wide_unit:]
                occ_weights = jnp.concatenate([occ * mask for mask in occ_mask], axis=0)
                virt_weights = jnp.concatenate(
                    [
                        jnp.broadcast_to(virt[nu : nu + 1], virt.shape) * virt_mask[unit]
                        for unit in range(CHUNK)
                        for nu in range(block_size)
                    ],
                    axis=0,
                )
                occupied = lax.dot_general(
                    rows_ref[atoms[member]],
                    occ_weights.astype(BF16),
                    (((0,), (0,)), ((), ())),
                    preferred_element_type=F32,
                ).astype(BF16)
                both = jnp.dot(
                    occupied, virt_weights.astype(BF16), preferred_element_type=F32
                ).astype(BF16)
                partner = []
                for unit in range(chunk * CHUNK, (chunk + 1) * CHUNK):
                    if unit < unit_count:
                        high = column_ref[step * group + member, 0, column_lane + unit]
                        low = column_ref[
                            step * group + member, 0, column_lane + unit_count + unit
                        ]
                        partner.append(rows_ref[high * BASE + low])
                    else:
                        partner.append(jnp.zeros((square, aux_count), BF16))
                total += jnp.dot(
                    both, jnp.concatenate(partner, axis=0), preferred_element_type=F32
                )
        return total

    steps = own_atoms // group
    total = jnp.zeros((aux_count, aux_count), F32)
    if steps == 1:
        total = work(0, total)
    else:
        total = lax.fori_loop(0, steps, work, total)
    row_count = keep_ref.shape[1]
    parts = [total[at * row_count : (at + 1) * row_count] for at in range(4)]
    keep = [jnp.where(half == 0, parts[2 * at], parts[2 * at + 1]) for at in range(2)]
    send = [jnp.where(half == 0, parts[2 * at + 1], parts[2 * at]) for at in range(2)]
    keep_ref[0] = jnp.where(outer == 0, keep[0], keep[1])
    keep_ref[1] = jnp.where(outer == 0, keep[1], keep[0])
    send_ref[0] = jnp.where(outer == 0, send[0], send[1])
    send_ref[1] = jnp.where(outer == 0, send[1], send[0])


VMEM = pl.BlockSpec(memory_space=pltpu.VMEM)
SMEM = pl.BlockSpec(memory_space=pltpu.SMEM)


def scalar(value):
    return value.astype(jnp.int32).reshape(1)


def gather_over_wide(block, wide_count, pair_count):
    if wide_count != 8:
        return [lax.all_gather(block, "wide", axis=0, tiled=True)], (None,)
    partner = [(p, p ^ 1) for p in range(pair_count)]
    blocks, offsets = [], []
    for even, odd in ((4, 5), (6, 7), (2, 3), (0, 1)):
        route = [
            ((w ^ d) * pair_count + p, w * pair_count + p)
            for w in range(wide_count)
            for p in range(pair_count)
            for d in (odd if p % 2 else even,)
            if d
        ]
        fetched = lax.ppermute(block, ("wide", "pair"), route)
        blocks += [fetched, lax.ppermute(fetched, "pair", partner)]
        offsets += [(even, odd), (odd, even)]
    return blocks + [block], tuple(offsets + [(0, 0)])


def local(three_center, occ_green, virt_green, occ_column, partner_live):
    local_atoms, block_size, wide_row = three_center.shape
    own_units = occ_green.shape[1]
    aux_count = wide_row // block_size
    wide_count, pair_count = lax.axis_size("wide"), lax.axis_size("pair")
    unit_count = 2 * own_units
    _, column_at, lanes = small_layout(unit_count, block_size)
    wide_at = scalar(lax.axis_index("wide"))
    pair_at = scalar(lax.axis_index("pair"))
    partner = [(p, p ^ 1) for p in range(pair_count)]

    block, small = pl.pallas_call(
        pack_kernel,
        out_shape=(
            pltpu.VMEM((local_atoms, block_size, wide_row + lanes), BF16),
            pltpu.VMEM((local_atoms, block_size, lanes), BF16),
        ),
        in_specs=[SMEM, SMEM, SMEM, VMEM, VMEM, VMEM],
        out_specs=(VMEM, VMEM),
        name="pack",
    )(pair_at, occ_column.T, partner_live.T, three_center, occ_green, virt_green)
    merged = small + lax.ppermute(small, "pair", partner)
    block = lax.dynamic_update_slice(block, merged, (0, 0, wide_row))
    blocks, offsets = gather_over_wide(block, wide_count, pair_count)
    if wide_count == 8:
        blocks = [pltpu.with_memory_space_constraint(block, pltpu.VMEM) for block in blocks]

    atom_total = wide_count * local_atoms
    own_atoms = atom_total // 2
    index_lanes = lanes - column_at // 128 * 128
    row_count = aux_count // pair_count
    part = pltpu.VMEM((2, row_count, aux_count), F32)
    keep, send = pl.pallas_call(
        functools.partial(response_kernel, wide_count, unit_count, offsets),
        out_shape=(part, part),
        in_specs=[SMEM, SMEM] + [VMEM] * len(blocks),
        out_specs=(VMEM, VMEM),
        scratch_shapes=[
            pltpu.VMEM((atom_total, block_size * block_size, aux_count), BF16),
            pltpu.VMEM((atom_total, block_size, lanes), BF16),
            pltpu.VMEM((own_atoms, 1, index_lanes), jnp.int32),
            pltpu.SMEM((own_atoms, 1, index_lanes), jnp.int32),
            pltpu.SemaphoreType.DMA,
        ],
        compiler_params=pltpu.CompilerParams(vmem_limit_bytes=56 * 2**20),
        name="response",
    )(wide_at, pair_at, *blocks)
    summed = keep + lax.ppermute(send, "pair", partner)
    other = [(p, p ^ 2) for p in range(pair_count)]
    return summed[0] + lax.ppermute(summed[1], "pair", other)


def solution(mesh):
    placed = (
        P("wide", None, None),
        P("wide", "pair", None, None),
        P("wide", "pair", None, None),
        P("wide", "pair"),
        P("wide", "pair"),
    )
    return jax.shard_map(
        local, mesh=mesh, in_specs=placed, out_specs=P("pair", None), check_vma=False
    )
```

```python
import functools

import jax
import jax.numpy as jnp
from jax import lax
from jax.experimental import pallas as pl
from jax.experimental.pallas import tpu as pltpu
from jax.sharding import PartitionSpec as P

CHUNK = 4
BASE = 256
F32, BF16 = jnp.float32, jnp.bfloat16


def ceil_to(value, step):
    return -(-value // step) * step


def small_layout(unit_count, block_size):
    chunk_count = -(-unit_count // CHUNK)
    column_at = chunk_count * 2 * CHUNK * block_size
    return chunk_count, column_at, ceil_to(column_at + 2 * unit_count, 128)


def iota(shape, axis):
    return lax.broadcasted_iota(jnp.int32, shape, axis)


def pack_kernel(pair_ref, column_ref, live_ref, tc_ref, occ_ref, virt_ref, block_ref, small_ref):
    local_atoms, own_units, block_size, _ = occ_ref.shape
    wide_row = tc_ref.shape[2]
    unit_count = 2 * own_units
    _, column_at, lanes = small_layout(unit_count, block_size)
    half = pair_ref[0] % 2
    row, lane = iota((block_size, lanes), 0), iota((block_size, lanes), 1)
    packed = jnp.zeros((local_atoms * block_size, lanes), F32)
    columns = [jnp.zeros((block_size, lanes), F32) for _ in range(local_atoms)]
    for slot in range(own_units):
        unit = half * own_units + slot
        at = (unit // CHUNK) * (2 * CHUNK * block_size) + (unit % CHUNK) * block_size
        occ = jnp.concatenate(
            [
                occ_ref[atom, slot].astype(F32) * live_ref[slot, atom].astype(F32)
                for atom in range(local_atoms)
            ],
            axis=0,
        ).astype(BF16)
        virt = jnp.concatenate(
            [virt_ref[atom, slot].astype(F32) for atom in range(local_atoms)], axis=0
        ).astype(BF16)
        occ_place = (lane == at + row).astype(BF16)
        virt_place = (lane == at + CHUNK * block_size + row).astype(BF16)
        packed += jnp.dot(occ, occ_place, preferred_element_type=F32)
        packed += jnp.dot(virt, virt_place, preferred_element_type=F32)
        for atom in range(local_atoms):
            column = column_ref[slot, atom]
            high = column // BASE
            low = column - high * BASE
            columns[atom] += jnp.where(lane == column_at + unit, high.astype(F32), 0.0)
            columns[atom] += jnp.where(
                lane == column_at + unit_count + unit, low.astype(F32), 0.0
            )
    packed = (packed + jnp.concatenate(columns, axis=0)).astype(BF16)
    packed = packed.reshape(local_atoms, block_size, lanes)
    block_ref[:, :, :wide_row] = tc_ref[...]
    block_ref[:, :, wide_row:] = packed
    small_ref[...] = packed


def response_kernel(wide_count, unit_count, offsets, wide_ref, pair_ref, *refs):
    block_refs = refs[: -9]
    keep_ref, send_ref, rows_ref, small_ref, index_ref, column_ref, sem, occupied_ref, both_ref = refs[-9:]
    block_size = block_refs[0].shape[1]
    square = block_size * block_size
    aux_count = rows_ref.shape[2]
    chunk_count, column_at, lanes = small_layout(unit_count, block_size)
    atom_total = rows_ref.shape[0]
    local_atoms = atom_total // wide_count
    side, half, outer = wide_ref[0], pair_ref[0] % 2, pair_ref[0] // 2

    for number, block_ref in enumerate(block_refs):
        first = 0
        if offsets[number] is not None:
            even, odd = offsets[number]
            first = (side ^ jnp.where(half == 0, even, odd)) * local_atoms

        def place_atom(atom, block_ref=block_ref, first=first):
            rows_ref[first + atom] = jnp.concatenate(
                [
                    block_ref[atom, :, at * aux_count : (at + 1) * aux_count]
                    for at in range(block_size)
                ],
                axis=0,
            )
            small_ref[first + atom] = block_ref[atom, :, block_size * aux_count :]

        if block_ref.shape[0] <= 8:
            for atom in range(block_ref.shape[0]):
                place_atom(atom)
        else:
            pl.loop(0, block_ref.shape[0])(place_atom)

    own_atoms = index_ref.shape[0]
    column_tile = column_at // 128 * 128
    column_lane = column_at - column_tile

    def atom_of(position):
        return ((position // local_atoms) * 2 + (side ^ half) % 2) * local_atoms + position % local_atoms

    def place_column(position):
        digits = small_ref[atom_of(position)][:, column_tile:].astype(F32)
        index_ref[position] = digits[0:1, :].astype(jnp.int32)

    if own_atoms <= 16:
        for position in range(own_atoms):
            place_column(position)
    else:
        pl.loop(0, own_atoms)(place_column)
    copy = pltpu.make_async_copy(index_ref, column_ref, sem)
    copy.start()

    wide_unit = CHUNK * square
    spread_row, spread_lane = iota((128, 2 * wide_unit), 0), iota((128, 2 * wide_unit), 1)
    is_virt = spread_lane >= wide_unit
    inner = spread_lane % wide_unit
    unit_of, upper, lower = inner // square, (inner // block_size) % block_size, inner % block_size
    wanted = unit_of * block_size + jnp.where(is_virt, upper + CHUNK * block_size, lower)
    lane_row, lane = iota((block_size, wide_unit), 0), iota((block_size, wide_unit), 1)
    lane_unit, lane_upper, lane_lower = lane // square, (lane // block_size) % block_size, lane % block_size
    occ_mask = [(lane_upper == at).astype(F32) for at in range(block_size)]
    virt_mask = [
        ((lane_unit == at) & (lane_lower == lane_row)).astype(F32) for at in range(CHUNK)
    ]
    group = max(1, min(own_atoms, 16 // chunk_count))
    copy.wait()

    def work(step, total):
        for chunk in range(chunk_count):
            at = chunk * 2 * CHUNK * block_size
            tile = at // 128 * 128
            spread = (spread_row == wanted + (at - tile)).astype(BF16)
            atoms = [atom_of(step * group + member) for member in range(group)]
            smalls = jnp.concatenate(
                [small_ref[atom][:, tile : tile + 128] for atom in atoms], axis=0
            )
            wide = jnp.dot(smalls, spread, preferred_element_type=F32)
            for member in range(group):
                occ = wide[member * block_size : (member + 1) * block_size, :wide_unit]
                occ_weights = jnp.concatenate([occ * mask for mask in occ_mask], axis=0)
                occupied_ref[:, member * wide_unit : (member + 1) * wide_unit] = lax.dot_general(
                    rows_ref[atoms[member]],
                    occ_weights.astype(BF16),
                    (((0,), (0,)), ((), ())),
                    preferred_element_type=F32,
                ).astype(BF16)
            for member in range(group):
                virt = wide[member * block_size : (member + 1) * block_size, wide_unit:]
                virt_weights = jnp.concatenate(
                    [
                        jnp.broadcast_to(virt[nu : nu + 1], virt.shape) * virt_mask[unit]
                        for unit in range(CHUNK)
                        for nu in range(block_size)
                    ],
                    axis=0,
                )
                both_ref[:, member * wide_unit : (member + 1) * wide_unit] = jnp.dot(
                    occupied_ref[:, member * wide_unit : (member + 1) * wide_unit],
                    virt_weights.astype(BF16), preferred_element_type=F32
                ).astype(BF16)
            partner = []
            for member in range(group):
                for unit in range(chunk * CHUNK, (chunk + 1) * CHUNK):
                    if unit < unit_count:
                        high = column_ref[step * group + member, 0, column_lane + unit]
                        low = column_ref[
                            step * group + member, 0, column_lane + unit_count + unit
                        ]
                        partner.append(rows_ref[high * BASE + low])
                    else:
                        partner.append(jnp.zeros((square, aux_count), BF16))
            total += jnp.dot(
                both_ref[...], jnp.concatenate(partner, axis=0), preferred_element_type=F32
            )
        return total

    steps = own_atoms // group
    total = jnp.zeros((aux_count, aux_count), F32)
    if steps == 1:
        total = work(0, total)
    else:
        total = lax.fori_loop(0, steps, work, total)
    row_count = keep_ref.shape[1]
    parts = [total[at * row_count : (at + 1) * row_count] for at in range(4)]
    keep = [jnp.where(half == 0, parts[2 * at], parts[2 * at + 1]) for at in range(2)]
    send = [jnp.where(half == 0, parts[2 * at + 1], parts[2 * at]) for at in range(2)]
    keep_ref[0] = jnp.where(outer == 0, keep[0], keep[1])
    keep_ref[1] = jnp.where(outer == 0, keep[1], keep[0])
    send_ref[0] = jnp.where(outer == 0, send[0], send[1])
    send_ref[1] = jnp.where(outer == 0, send[1], send[0])


VMEM = pl.BlockSpec(memory_space=pltpu.VMEM)
SMEM = pl.BlockSpec(memory_space=pltpu.SMEM)


def scalar(value):
    return value.astype(jnp.int32).reshape(1)


def gather_over_wide(block, wide_count, pair_count):
    if wide_count != 8:
        return [lax.all_gather(block, "wide", axis=0, tiled=True)], (None,)
    partner = [(p, p ^ 1) for p in range(pair_count)]
    blocks, offsets = [], []
    for even, odd in ((0, 1), (2, 3), (6, 7), (4, 5)):
        route = [
            ((w ^ d) * pair_count + p, w * pair_count + p)
            for w in range(wide_count)
            for p in range(pair_count)
            for d in (odd if p % 2 else even,)
            if d
        ]
        fetched = lax.ppermute(block, ("wide", "pair"), route)
        blocks += [fetched, lax.ppermute(fetched, "pair", partner)]
        offsets += [(even, odd), (odd, even)]
    return blocks + [block], tuple(offsets + [(0, 0)])


def local(three_center, occ_green, virt_green, occ_column, partner_live):
    local_atoms, block_size, wide_row = three_center.shape
    own_units = occ_green.shape[1]
    aux_count = wide_row // block_size
    wide_count, pair_count = lax.axis_size("wide"), lax.axis_size("pair")
    unit_count = 2 * own_units
    _, column_at, lanes = small_layout(unit_count, block_size)
    wide_at = scalar(lax.axis_index("wide"))
    pair_at = scalar(lax.axis_index("pair"))
    partner = [(p, p ^ 1) for p in range(pair_count)]

    block, small = pl.pallas_call(
        pack_kernel,
        out_shape=(
            pltpu.VMEM((local_atoms, block_size, wide_row + lanes), BF16),
            pltpu.VMEM((local_atoms, block_size, lanes), BF16),
        ),
        in_specs=[SMEM, SMEM, SMEM, VMEM, VMEM, VMEM],
        out_specs=(VMEM, VMEM),
        name="pack",
    )(pair_at, occ_column.T, partner_live.T, three_center, occ_green, virt_green)
    merged = small + lax.ppermute(small, "pair", partner)
    block = lax.dynamic_update_slice(block, merged, (0, 0, wide_row))
    blocks, offsets = gather_over_wide(block, wide_count, pair_count)
    if wide_count == 8:
        blocks = [pltpu.with_memory_space_constraint(block, pltpu.VMEM) for block in blocks]

    atom_total = wide_count * local_atoms
    own_atoms = atom_total // 2
    group_lanes = max(1, min(own_atoms, 16 // -(-unit_count // CHUNK))) * CHUNK * block_size**2
    index_lanes = lanes - column_at // 128 * 128
    row_count = aux_count // pair_count
    part = pltpu.VMEM((2, row_count, aux_count), F32)
    keep, send = pl.pallas_call(
        functools.partial(response_kernel, wide_count, unit_count, offsets),
        out_shape=(part, part),
        in_specs=[SMEM, SMEM] + [VMEM] * len(blocks),
        out_specs=(VMEM, VMEM),
        scratch_shapes=[
            pltpu.VMEM((atom_total, block_size * block_size, aux_count), BF16),
            pltpu.VMEM((atom_total, block_size, lanes), BF16),
            pltpu.VMEM((own_atoms, 1, index_lanes), jnp.int32),
            pltpu.SMEM((own_atoms, 1, index_lanes), jnp.int32),
            pltpu.SemaphoreType.DMA,
            pltpu.VMEM((aux_count, group_lanes), BF16),
            pltpu.VMEM((aux_count, group_lanes), BF16),
        ],
        compiler_params=pltpu.CompilerParams(vmem_limit_bytes=56 * 2**20),
        name="response",
    )(wide_at, pair_at, *blocks)
    summed = keep + lax.ppermute(send, "pair", partner)
    other = [(p, p ^ 2) for p in range(pair_count)]
    return summed[0] + lax.ppermute(summed[1], "pair", other)


def solution(mesh):
    placed = (
        P("wide", None, None),
        P("wide", "pair", None, None),
        P("wide", "pair", None, None),
        P("wide", "pair"),
        P("wide", "pair"),
    )
    return jax.shard_map(
        local, mesh=mesh, in_specs=placed, out_specs=P("pair", None), check_vma=False
    )
```

```python
import functools

import jax
import jax.numpy as jnp
from jax import lax
from jax.experimental import pallas as pl
from jax.experimental.pallas import tpu as pltpu
from jax.sharding import PartitionSpec as P

CHUNK = 4
BASE = 256
F32, BF16 = jnp.float32, jnp.bfloat16


def ceil_to(value, step):
    return -(-value // step) * step


def small_layout(unit_count, block_size):
    chunk_count = -(-unit_count // CHUNK)
    column_at = chunk_count * 2 * CHUNK * block_size
    return chunk_count, column_at, ceil_to(column_at + 2 * unit_count, 128)


def iota(shape, axis):
    return lax.broadcasted_iota(jnp.int32, shape, axis)


def pack_kernel(pair_ref, column_ref, live_ref, tc_ref, occ_ref, virt_ref, block_ref, small_ref):
    local_atoms, own_units, block_size, _ = occ_ref.shape
    wide_row = tc_ref.shape[2]
    unit_count = 2 * own_units
    _, column_at, lanes = small_layout(unit_count, block_size)
    half = pair_ref[0] % 2
    row, lane = iota((block_size, lanes), 0), iota((block_size, lanes), 1)
    packed = jnp.zeros((local_atoms * block_size, lanes), F32)
    columns = [jnp.zeros((block_size, lanes), F32) for _ in range(local_atoms)]
    for slot in range(own_units):
        unit = half * own_units + slot
        at = (unit // CHUNK) * (2 * CHUNK * block_size) + (unit % CHUNK) * block_size
        occ = jnp.concatenate(
            [
                occ_ref[atom, slot].astype(F32) * live_ref[slot, atom].astype(F32)
                for atom in range(local_atoms)
            ],
            axis=0,
        ).astype(BF16)
        virt = jnp.concatenate(
            [virt_ref[atom, slot].astype(F32) for atom in range(local_atoms)], axis=0
        ).astype(BF16)
        occ_place = (lane == at + row).astype(BF16)
        virt_place = (lane == at + CHUNK * block_size + row).astype(BF16)
        packed += jnp.dot(occ, occ_place, preferred_element_type=F32)
        packed += jnp.dot(virt, virt_place, preferred_element_type=F32)
        for atom in range(local_atoms):
            column = column_ref[slot, atom]
            high = column // BASE
            low = column - high * BASE
            columns[atom] += jnp.where(lane == column_at + unit, high.astype(F32), 0.0)
            columns[atom] += jnp.where(
                lane == column_at + unit_count + unit, low.astype(F32), 0.0
            )
    packed = (packed + jnp.concatenate(columns, axis=0)).astype(BF16)
    packed = packed.reshape(local_atoms, block_size, lanes)
    block_ref[:, :, :wide_row] = tc_ref[...]
    block_ref[:, :, wide_row:] = packed
    small_ref[...] = packed


def in_rows(block, aux_count):
    parts = range(block.shape[0])
    return jnp.concatenate([block[:, at * aux_count : (at + 1) * aux_count] for at in parts], axis=0)


def digits_of(small, column_at):
    digits = small[:, column_at // 128 * 128 :].astype(F32)
    return digits[0:1, :].astype(jnp.int32)


def weight_parts(block_size, lane_at):
    square = block_size * block_size
    wide_unit = CHUNK * square
    row, lane = iota((128, 2 * wide_unit), 0), iota((128, 2 * wide_unit), 1)
    inner = lane % wide_unit
    unit, upper, lower = inner // square, (inner // block_size) % block_size, inner % block_size
    within = jnp.where(lane >= wide_unit, upper + CHUNK * block_size, lower)
    spread = (row == unit * block_size + within + lane_at).astype(BF16)
    row, lane = iota((block_size, wide_unit), 0), iota((block_size, wide_unit), 1)
    unit, upper, lower = lane // square, (lane // block_size) % block_size, lane % block_size
    occ_mask = [(upper == at).astype(F32) for at in range(block_size)]
    virt_mask = [((unit == at) & (lower == row)).astype(F32) for at in range(CHUNK)]
    return spread, occ_mask, virt_mask


def contract(rows, smalls, parts, occupied_ref, both_ref):
    spread, occ_mask, virt_mask = parts
    block_size, wide_unit = occ_mask[0].shape
    wide = jnp.dot(jnp.concatenate(smalls, axis=0), spread, preferred_element_type=F32)
    for member in range(len(rows)):
        occ = wide[member * block_size : (member + 1) * block_size, :wide_unit]
        weights = jnp.concatenate([occ * mask for mask in occ_mask], axis=0)
        occupied_ref[:, member * wide_unit : (member + 1) * wide_unit] = lax.dot_general(
            rows[member],
            weights.astype(BF16),
            (((0,), (0,)), ((), ())),
            preferred_element_type=F32,
        ).astype(BF16)
    for member in range(len(rows)):
        virt = wide[member * block_size : (member + 1) * block_size, wide_unit:]
        weights = jnp.concatenate(
            [
                jnp.broadcast_to(virt[nu : nu + 1], virt.shape) * mask
                for mask in virt_mask
                for nu in range(block_size)
            ],
            axis=0,
        )
        at = slice(member * wide_unit, (member + 1) * wide_unit)
        both_ref[:, at] = jnp.dot(
            occupied_ref[:, at], weights.astype(BF16), preferred_element_type=F32
        ).astype(BF16)


def partner_rows(rows_ref, columns, unit_count, chunk):
    found = []
    for unit in range(chunk * CHUNK, (chunk + 1) * CHUNK):
        if unit < unit_count:
            found.append(rows_ref[columns(unit) * BASE + columns(unit_count + unit)])
        else:
            found.append(jnp.zeros(rows_ref.shape[1:], BF16))
    return found


def write_rows(total, pair_at, keep_ref, send_ref):
    half, outer = pair_at % 2, pair_at // 2
    row_count = keep_ref.shape[1]
    parts = [total[at * row_count : (at + 1) * row_count] for at in range(4)]
    keep = [jnp.where(half == 0, parts[2 * at], parts[2 * at + 1]) for at in range(2)]
    send = [jnp.where(half == 0, parts[2 * at + 1], parts[2 * at]) for at in range(2)]
    for ref, both in ((keep_ref, keep), (send_ref, send)):
        ref[0] = jnp.where(outer == 0, both[0], both[1])
        ref[1] = jnp.where(outer == 0, both[1], both[0])


def contract_kernel(unit_count, wide_ref, pair_ref, own_ref, *refs):
    count = len(PAIRS)
    block_refs = refs[:count]
    both_ref, rows_ref, index_ref, occupied_ref, small_ref = refs[count:]
    local_atoms, block_size, _ = own_ref.shape
    aux_count = both_ref.shape[0]
    _, column_at, lanes = small_layout(unit_count, block_size)
    side, half = wide_ref[0], pair_ref[0] % 2
    for slot, (even, odd) in enumerate(PAIRS):
        place = (side ^ jnp.where(half == 0, even, odd)) // 2 * local_atoms
        for atom in range(local_atoms):
            block = block_refs[slot][atom]
            if even == 0:
                block = jnp.where(half == 0, own_ref[atom], block)
            rows_ref[place + atom] = in_rows(block, aux_count)
            small_ref[place + atom] = block[:, block_size * aux_count :]
    atoms = range(count * local_atoms)
    smalls = [small_ref[atom] for atom in atoms]
    row, lane = iota((lanes, 128), 0), iota((lanes, 128), 1)
    join = jnp.where(row == column_at + lane, float(BASE), 0.0)
    join += jnp.where(row == column_at + unit_count + lane, 1.0, 0.0)
    joined = jnp.dot(
        jnp.concatenate(smalls, axis=0), join.astype(BF16), preferred_element_type=F32
    ).astype(jnp.int32)
    contract(
        [rows_ref[atom] for atom in atoms], smalls, weight_parts(block_size, 0), occupied_ref, both_ref
    )
    for atom in atoms:
        for unit in range(unit_count):
            index_ref[atom, unit] = joined[atom * block_size, unit]


def respond_kernel(unit_count, wide_ref, pair_ref, index_ref, own_ref, both_ref, near_ref, *refs):
    count = len(PAIRS)
    far_refs = refs[:count]
    keep_ref, send_ref, rows_ref = refs[count:]
    local_atoms, block_size, _ = own_ref.shape
    aux_count = rows_ref.shape[2]
    side, half = wide_ref[0], pair_ref[0] % 2
    for slot, (even, odd) in enumerate(PAIRS):
        owner = side ^ jnp.where(half == 0, odd, even)
        for atom in range(local_atoms):
            rows_ref[owner * local_atoms + atom] = in_rows(far_refs[slot][atom], aux_count)
    for atom in range(local_atoms):
        rows_ref[side * local_atoms + atom] = in_rows(own_ref[atom], aux_count)
    for place in range(count):
        owner = place * 2 + (side ^ half) % 2
        for atom in range(local_atoms):
            rows_ref[owner * local_atoms + atom] = near_ref[place * local_atoms + atom]
    found = []
    for atom in range(count * local_atoms):
        for unit in range(CHUNK):
            if unit < unit_count:
                found.append(rows_ref[index_ref[atom, unit]])
            else:
                found.append(jnp.zeros(rows_ref.shape[1:], BF16))
    total = jnp.dot(both_ref[...], jnp.concatenate(found, axis=0), preferred_element_type=F32)
    write_rows(total, pair_ref[0], keep_ref, send_ref)


def whole_kernel(wide_count, unit_count, pair_ref, block_ref, *refs):
    keep_ref, send_ref, rows_ref, index_ref, column_ref, occupied_ref, both_ref, sem = refs
    atom_total, block_size, _ = block_ref.shape
    aux_count = rows_ref.shape[2]
    local_atoms = atom_total // wide_count
    chunk_count, column_at, _ = small_layout(unit_count, block_size)
    column_lane = column_at % 128
    half = pair_ref[0] % 2
    group = both_ref.shape[1] // (CHUNK * block_size * block_size)

    def atom_of(position):
        return (position // local_atoms * 2 + half) * local_atoms + position % local_atoms

    @pl.loop(0, atom_total)
    def _(atom):
        rows_ref[atom] = in_rows(block_ref[atom], aux_count)
        index_ref[atom] = digits_of(block_ref[atom, :, block_size * aux_count :], column_at)

    copy = pltpu.make_async_copy(index_ref, column_ref, sem)
    copy.start()
    copy.wait()

    def work(step, total):
        atoms = [atom_of(step * group + member) for member in range(group)]
        for chunk in range(chunk_count):
            lane_at = chunk * 2 * CHUNK * block_size
            tile = block_size * aux_count + lane_at // 128 * 128
            parts = weight_parts(block_size, lane_at % 128)
            smalls = [block_ref[atom, :, tile : tile + 128] for atom in atoms]
            contract([rows_ref[atom] for atom in atoms], smalls, parts, occupied_ref, both_ref)
            found = []
            for atom in atoms:
                found += partner_rows(
                    rows_ref, lambda lane: column_ref[atom, 0, column_lane + lane], unit_count, chunk
                )
            total += jnp.dot(
                both_ref[...], jnp.concatenate(found, axis=0), preferred_element_type=F32
            )
        return total

    total = jnp.zeros((aux_count, aux_count), F32)
    total = lax.fori_loop(0, atom_total // 2 // group, work, total)
    write_rows(total, pair_ref[0], keep_ref, send_ref)


VMEM = pl.BlockSpec(memory_space=pltpu.VMEM)
SMEM = pl.BlockSpec(memory_space=pltpu.SMEM)


def scalar(value):
    return value.astype(jnp.int32).reshape(1)


PAIRS = ((4, 5), (6, 7), (2, 3), (0, 1))


def respond_direct(block, wide_at, pair_at, unit_count, wide_count, pair_count, aux_count):
    local_atoms, block_size, width = block.shape
    square = block_size * block_size
    partner = [(p, p ^ 1) for p in range(pair_count)]
    fetched, far = [], []
    for even, odd in PAIRS:
        route = [
            ((w ^ d) * pair_count + p, w * pair_count + p)
            for w in range(wide_count)
            for p in range(pair_count)
            for d in (odd if p % 2 else even,)
            if d
        ]
        fetched.append(lax.ppermute(block, ("wide", "pair"), route))
        far.append(lax.ppermute(fetched[-1], "pair", partner))
    near_atoms = len(PAIRS) * local_atoms
    both, near, index = pl.pallas_call(
        functools.partial(contract_kernel, unit_count),
        out_shape=(
            pltpu.VMEM((aux_count, near_atoms * CHUNK * square), BF16),
            pltpu.VMEM((near_atoms, square, aux_count), BF16),
            pltpu.SMEM((near_atoms, unit_count), jnp.int32),
        ),
        in_specs=[SMEM, SMEM] + [VMEM] * (1 + len(PAIRS)),
        out_specs=(VMEM, VMEM, SMEM),
        scratch_shapes=[
            pltpu.VMEM((aux_count, near_atoms * CHUNK * square), BF16),
            pltpu.VMEM((near_atoms, block_size, width - block_size * aux_count), BF16),
        ],
        name="contract",
    )(wide_at, pair_at, *[in_vmem(value) for value in [block] + fetched])
    part = pltpu.VMEM((2, aux_count // pair_count, aux_count), F32)
    return pl.pallas_call(
        functools.partial(respond_kernel, unit_count),
        out_shape=(part, part),
        in_specs=[SMEM, SMEM, SMEM] + [VMEM] * (3 + len(PAIRS)),
        out_specs=(VMEM, VMEM),
        scratch_shapes=[pltpu.VMEM((wide_count * local_atoms, square, aux_count), BF16)],
        name="respond",
    )(
        wide_at,
        pair_at,
        pltpu.with_memory_space_constraint(index, pltpu.SMEM),
        *[in_vmem(value) for value in [block, both, near] + far],
    )


def respond_whole(block, pair_at, unit_count, wide_count, pair_count, aux_count):
    local_atoms, block_size, width = block.shape
    square = block_size * block_size
    chunk_count, column_at, _ = small_layout(unit_count, block_size)
    index_lanes = width - block_size * aux_count - column_at // 128 * 128
    atom_total = wide_count * local_atoms
    group = max(1, min(local_atoms, 16 // chunk_count))
    group_lanes = group * CHUNK * square
    part = pltpu.VMEM((2, aux_count // pair_count, aux_count), F32)
    return pl.pallas_call(
        functools.partial(whole_kernel, wide_count, unit_count),
        out_shape=(part, part),
        in_specs=[SMEM, VMEM],
        out_specs=(VMEM, VMEM),
        scratch_shapes=[
            pltpu.VMEM((atom_total, square, aux_count), BF16),
            pltpu.VMEM((atom_total, 1, index_lanes), jnp.int32),
            pltpu.SMEM((atom_total, 1, index_lanes), jnp.int32),
            pltpu.VMEM((aux_count, group_lanes), BF16),
            pltpu.VMEM((aux_count, group_lanes), BF16),
            pltpu.SemaphoreType.DMA,
        ],
        compiler_params=pltpu.CompilerParams(vmem_limit_bytes=56 * 2**20),
        name="whole",
    )(pair_at, lax.all_gather(block, "wide", axis=0, tiled=True))


def in_vmem(value):
    return pltpu.with_memory_space_constraint(value, pltpu.VMEM)


def local(three_center, occ_green, virt_green, occ_column, partner_live):
    local_atoms, block_size, wide_row = three_center.shape
    own_units = occ_green.shape[1]
    aux_count = wide_row // block_size
    wide_count, pair_count = lax.axis_size("wide"), lax.axis_size("pair")
    unit_count = 2 * own_units
    _, _, lanes = small_layout(unit_count, block_size)
    wide_at = scalar(lax.axis_index("wide"))
    pair_at = scalar(lax.axis_index("pair"))
    partner = [(p, p ^ 1) for p in range(pair_count)]

    block, small = pl.pallas_call(
        pack_kernel,
        out_shape=(
            pltpu.VMEM((local_atoms, block_size, wide_row + lanes), BF16),
            pltpu.VMEM((local_atoms, block_size, lanes), BF16),
        ),
        in_specs=[SMEM, SMEM, SMEM, VMEM, VMEM, VMEM],
        out_specs=(VMEM, VMEM),
        name="pack",
    )(pair_at, occ_column.T, partner_live.T, three_center, occ_green, virt_green)
    merged = small + lax.ppermute(small, "pair", partner)
    block = lax.dynamic_update_slice(block, merged, (0, 0, wide_row))
    if wide_count == 8 and unit_count <= CHUNK:
        keep, send = respond_direct(
            block, wide_at, pair_at, unit_count, wide_count, pair_count, aux_count
        )
    else:
        keep, send = respond_whole(block, pair_at, unit_count, wide_count, pair_count, aux_count)
    summed = keep + lax.ppermute(send, "pair", partner)
    other = [(p, p ^ 2) for p in range(pair_count)]
    return summed[0] + lax.ppermute(summed[1], "pair", other)


def solution(mesh):
    placed = (
        P("wide", None, None),
        P("wide", "pair", None, None),
        P("wide", "pair", None, None),
        P("wide", "pair"),
        P("wide", "pair"),
    )
    return jax.shard_map(
        local, mesh=mesh, in_specs=placed, out_specs=P("pair", None), check_vma=False
    )
```

```python
import jax
import jax.numpy as jnp
from jax import lax
from jax.experimental import pallas as pl
from jax.experimental.pallas import tpu as pltpu
from jax.sharding import PartitionSpec as P

CHUNK = 4
BASE = 256
PAIRS = ((4, 5), (6, 7), (0, 1), (2, 3))
F32, BF16 = jnp.float32, jnp.bfloat16
VMEM = pl.BlockSpec(memory_space=pltpu.VMEM)
SMEM = pl.BlockSpec(memory_space=pltpu.SMEM)


def ceil_to(value, step):
    return -(-value // step) * step


def iota(shape, axis):
    return lax.broadcasted_iota(jnp.int32, shape, axis)


def scalar(value):
    return value.astype(jnp.int32).reshape(1)


def in_vmem(value):
    return pltpu.with_memory_space_constraint(value, pltpu.VMEM)


def small_layout(unit_count, block_size):
    chunk_count = -(-unit_count // CHUNK)
    column_at = ceil_to(chunk_count * 2 * CHUNK * block_size, 128)
    return chunk_count, column_at, ceil_to(column_at + 2 * unit_count, 128)


def pack_kernel(unit_count, pair_ref, column_ref, live_ref, tc_ref, occ_ref, virt_ref, block_ref, small_ref):
    local_atoms, own_units, block_size, _ = occ_ref.shape
    wide_row = tc_ref.shape[2]
    _, column_at, lanes = small_layout(unit_count, block_size)
    row, lane = iota((block_size, lanes), 0), iota((block_size, lanes), 1)
    packed = jnp.zeros((local_atoms * block_size, lanes), F32)
    columns = [jnp.zeros((block_size, lanes), F32) for _ in range(local_atoms)]
    for slot in range(own_units):
        unit = pair_ref[0] * own_units + slot
        at = (unit // CHUNK) * (2 * CHUNK * block_size) + (unit % CHUNK) * block_size
        occ = jnp.concatenate(
            [
                occ_ref[atom, slot].astype(F32) * live_ref[slot, atom].astype(F32)
                for atom in range(local_atoms)
            ],
            axis=0,
        ).astype(BF16)
        virt = jnp.concatenate(
            [virt_ref[atom, slot].astype(F32) for atom in range(local_atoms)], axis=0
        ).astype(BF16)
        occ_place = (lane == at + row).astype(BF16)
        virt_place = (lane == at + CHUNK * block_size + row).astype(BF16)
        packed += jnp.dot(occ, occ_place, preferred_element_type=F32)
        packed += jnp.dot(virt, virt_place, preferred_element_type=F32)
        for atom in range(local_atoms):
            column = column_ref[slot, atom]
            high = column // BASE
            low = column - high * BASE
            columns[atom] += jnp.where(lane == column_at + unit, high.astype(F32), 0.0)
            columns[atom] += jnp.where(
                lane == column_at + unit_count + unit, low.astype(F32), 0.0
            )
    packed = (packed + jnp.concatenate(columns, axis=0)).astype(BF16)
    packed = packed.reshape(local_atoms, block_size, lanes)
    block_ref[:, :, :wide_row] = tc_ref[...]
    block_ref[:, :, wide_row:] = packed
    small_ref[...] = packed


def in_rows(block, aux_count):
    parts = range(block.shape[0])
    return jnp.concatenate([block[:, at * aux_count : (at + 1) * aux_count] for at in parts], axis=0)


def own_rows(rows, outer, row_count):
    found = rows[:, :row_count]
    for at in range(1, rows.shape[1] // row_count):
        found = jnp.where(outer == at, rows[:, at * row_count : (at + 1) * row_count], found)
    return found


def turned(rows):
    found = []
    for at in range(0, len(rows), 2):
        both = jnp.concatenate(rows[at : at + 2], axis=1).T
        found += jnp.split(both, len(rows[at : at + 2]), axis=0)
    return found


def weight_parts(block_size, lane_at):
    square = block_size * block_size
    wide_unit = CHUNK * square
    row, lane = iota((128, 2 * wide_unit), 0), iota((128, 2 * wide_unit), 1)
    inner = lane % wide_unit
    unit, upper, lower = inner // square, (inner // block_size) % block_size, inner % block_size
    within = jnp.where(lane >= wide_unit, upper + CHUNK * block_size, lower)
    spread = (row == unit * block_size + within + lane_at).astype(BF16)
    row, lane = iota((block_size, wide_unit), 0), iota((block_size, wide_unit), 1)
    unit, upper, lower = lane // square, (lane // block_size) % block_size, lane % block_size
    occ_mask = [(upper == at).astype(F32) for at in range(block_size)]
    virt_mask = [((unit == at) & (lower == row)).astype(F32) for at in range(CHUNK)]
    return spread, occ_mask, virt_mask


def contract(rows, smalls, parts, occupied_ref, both_ref, first):
    spread, occ_mask, virt_mask = parts
    block_size, wide_unit = occ_mask[0].shape
    wide = jnp.dot(jnp.concatenate(smalls, axis=0), spread, preferred_element_type=F32)
    for member in range(len(rows)):
        occ = wide[member * block_size : (member + 1) * block_size, :wide_unit]
        weights = jnp.concatenate([occ * mask for mask in occ_mask], axis=0)
        at = slice(first + member * wide_unit, first + (member + 1) * wide_unit)
        occupied_ref[:, at] = jnp.dot(
            rows[member], weights.astype(BF16), preferred_element_type=F32
        ).astype(BF16)
    for member in range(len(rows)):
        virt = wide[member * block_size : (member + 1) * block_size, wide_unit:]
        half = wide_unit // 2
        for part in range(2):
            some = virt[:, part * half : (part + 1) * half]
            weights = jnp.concatenate(
                [
                    jnp.broadcast_to(some[nu : nu + 1], some.shape) * mask[:, :half]
                    for mask in virt_mask[: CHUNK // 2]
                    for nu in range(block_size)
                ],
                axis=0,
            )
            at = first + member * wide_unit + part * half
            both_ref[:, at : at + half] = jnp.dot(
                occupied_ref[:, at : at + half], weights.astype(BF16), preferred_element_type=F32
            ).astype(BF16)


def join_columns(digits, unit_count):
    row, lane = (iota((digits.shape[1], ceil_to(unit_count, 128)), axis) for axis in range(2))
    join = jnp.where(row == lane, float(BASE), 0.0) + jnp.where(row == unit_count + lane, 1.0, 0.0)
    join = jnp.where(lane < unit_count, join, 0.0).astype(BF16)
    return jnp.dot(digits, join, preferred_element_type=F32).astype(jnp.int32)


def write_rows(total, half, keep_ref, send_ref):
    row_count = keep_ref.shape[0]
    keep_ref[...] = jnp.where(half == 0, total[:row_count], total[row_count:])
    send_ref[...] = jnp.where(half == 0, total[row_count:], total[:row_count])


def kernel_of(function, *sizes):
    def kernel(*refs):
        function(*sizes, *refs)

    return kernel


def contract_kernel(unit_count, wide_ref, pair_ref, own_ref, early_ref, *refs):
    count = len(PAIRS)
    block_refs = refs[:count]
    both_ref, rows_ref, index_ref, occupied_ref, small_ref = refs[count:]
    local_atoms, block_size, _ = own_ref.shape
    aux_count, row_count = rows_ref.shape[2], both_ref.shape[0]
    chunk_count, column_at, lanes = small_layout(unit_count, block_size)
    side, half, outer = wide_ref[0], pair_ref[0] % 2, pair_ref[0] // 2
    for slot, (even, odd) in enumerate(PAIRS):
        place = (side ^ jnp.where(half == 0, even, odd)) // 2 * local_atoms
        for atom in range(local_atoms):
            block = block_refs[slot][atom]
            if even == 0:
                block = jnp.where(half == 0, own_ref[atom], block)
            rows_ref[place + atom] = in_rows(block, aux_count)
            small = block[:, block_size * aux_count :]
            small_ref[place + atom] = early_ref[atom] if slot == 0 else small
    atoms = range(count * local_atoms)
    rows = turned([own_rows(rows_ref[atom], outer, row_count) for atom in atoms])
    for chunk in range(chunk_count):
        lane_at = chunk * 2 * CHUNK * block_size
        tile = lane_at // 128 * 128
        smalls = [small_ref[atom, :, tile : tile + 128] for atom in atoms]
        first = chunk * len(atoms) * CHUNK * block_size * block_size
        contract(
            rows, smalls, weight_parts(block_size, lane_at - tile), occupied_ref, both_ref, first
        )
    digits = jnp.concatenate([small_ref[atom, :, column_at:] for atom in atoms], axis=0)
    joined = join_columns(digits, unit_count)
    for atom in atoms:
        for unit in range(unit_count):
            index_ref[atom, unit] = joined[atom * block_size, unit]


def respond_kernel(unit_count, wide_ref, pair_ref, index_ref, own_ref, both_ref, near_ref, *refs):
    count = len(PAIRS)
    far_refs = refs[:count]
    keep_ref, send_ref, rows_ref = refs[count:]
    local_atoms, block_size, _ = own_ref.shape
    aux_count = rows_ref.shape[2]
    chunk_count, _, _ = small_layout(unit_count, block_size)
    side, half = wide_ref[0], pair_ref[0] % 2
    for slot, (even, odd) in enumerate(PAIRS):
        owner = side ^ jnp.where(half == 0, odd, even)
        for atom in range(local_atoms):
            rows_ref[owner * local_atoms + atom] = in_rows(far_refs[slot][atom], aux_count)
    for atom in range(local_atoms):
        rows_ref[side * local_atoms + atom] = in_rows(own_ref[atom], aux_count)
    for place in range(count):
        owner = place * 2 + (side ^ half) % 2
        for atom in range(local_atoms):
            rows_ref[owner * local_atoms + atom] = near_ref[place * local_atoms + atom]
    found = []
    for chunk in range(chunk_count):
        for atom in range(count * local_atoms):
            for unit in range(chunk * CHUNK, (chunk + 1) * CHUNK):
                if unit < unit_count:
                    found.append(rows_ref[index_ref[atom, unit]])
                else:
                    found.append(jnp.zeros(rows_ref.shape[1:], BF16))
    total = jnp.dot(both_ref[...], jnp.concatenate(found, axis=0), preferred_element_type=F32)
    write_rows(total, half, keep_ref, send_ref)


def whole_kernel(wide_count, unit_count, pair_ref, block_ref, *refs):
    keep_ref, send_ref, rows_ref, occupied_ref, both_ref = refs
    atom_total, block_size, _ = block_ref.shape
    aux_count = rows_ref.shape[2]
    row_count = both_ref.shape[0]
    local_atoms = atom_total // wide_count
    chunk_count, column_at, _ = small_layout(unit_count, block_size)
    half, outer = pair_ref[0] % 2, pair_ref[0] // 2
    group = both_ref.shape[1] // (CHUNK * block_size * block_size)

    @pl.loop(0, atom_total)
    def _(atom):
        rows_ref[atom] = in_rows(block_ref[atom], aux_count)

    def work(step, total):
        positions = [step * group + member for member in range(group)]
        atoms = [(at // local_atoms * 2 + half) * local_atoms + at % local_atoms for at in positions]
        rows = turned([own_rows(rows_ref[atom], outer, row_count) for atom in atoms])
        column_tile = block_size * aux_count + column_at
        digits = jnp.concatenate([block_ref[atom, :, column_tile:] for atom in atoms], axis=0)
        joined = join_columns(digits, unit_count)
        for chunk in range(chunk_count):
            lane_at = chunk * 2 * CHUNK * block_size
            tile = block_size * aux_count + lane_at // 128 * 128
            smalls = [block_ref[atom, :, tile : tile + 128] for atom in atoms]
            contract(rows, smalls, weight_parts(block_size, lane_at % 128), occupied_ref, both_ref, 0)
            found = []
            for member in range(group):
                for unit in range(chunk * CHUNK, (chunk + 1) * CHUNK):
                    if unit < unit_count:
                        found.append(rows_ref[joined[member * block_size, unit]])
                    else:
                        found.append(jnp.zeros(rows_ref.shape[1:], BF16))
            total += jnp.dot(
                both_ref[...], jnp.concatenate(found, axis=0), preferred_element_type=F32
            )
        return total

    total = jnp.zeros((row_count, aux_count), F32)
    total = lax.fori_loop(0, atom_total // 2 // group, work, total)
    write_rows(total, half, keep_ref, send_ref)


def respond_direct(early, full, early_small, wide_at, pair_at, unit_count, sizes):
    wide_count, pair_count, aux_count = sizes
    local_atoms, block_size, _ = full.shape
    square = block_size * block_size
    partner = [(p, p ^ 1) for p in range(pair_count)]
    across = [(p, p ^ 2) for p in range(pair_count)]
    fetched, far = [], []
    for slot, (even, odd) in enumerate(PAIRS):
        route = [
            ((w ^ d) * pair_count + p, w * pair_count + p)
            for w in range(wide_count)
            for p in range(pair_count)
            for d in (odd if p % 2 else even,)
            if d
        ]
        fetched.append(lax.ppermute(full if slot else early, ("wide", "pair"), route))
        far.append(lax.ppermute(fetched[-1], "pair", partner))
    small = fetched[0][:, :, block_size * aux_count :]
    small = small + lax.ppermute(small, "pair", across)
    chunk_count, _, lanes = small_layout(unit_count, block_size)
    near_atoms = len(PAIRS) * local_atoms
    row_count = aux_count * 2 // pair_count
    width = near_atoms * chunk_count * CHUNK * square
    both, near, index = pl.pallas_call(
        kernel_of(contract_kernel, unit_count),
        out_shape=(
            pltpu.VMEM((row_count, width), BF16),
            pltpu.VMEM((near_atoms, square, aux_count), BF16),
            pltpu.SMEM((near_atoms, unit_count), jnp.int32),
        ),
        in_specs=[SMEM, SMEM] + [VMEM] * (2 + len(PAIRS)),
        out_specs=(VMEM, VMEM, SMEM),
        scratch_shapes=[
            pltpu.VMEM((row_count, width), BF16),
            pltpu.VMEM((near_atoms, block_size, lanes), BF16),
        ],
        name="contract",
    )(wide_at, pair_at, *[in_vmem(value) for value in [full, small] + fetched])
    part = pltpu.VMEM((row_count // 2, aux_count), F32)
    return pl.pallas_call(
        kernel_of(respond_kernel, unit_count),
        out_shape=(part, part),
        in_specs=[SMEM, SMEM, SMEM] + [VMEM] * (3 + len(PAIRS)),
        out_specs=(VMEM, VMEM),
        scratch_shapes=[pltpu.VMEM((wide_count * local_atoms, square, aux_count), BF16)],
        name="respond",
    )(
        wide_at,
        pair_at,
        pltpu.with_memory_space_constraint(index, pltpu.SMEM),
        *[in_vmem(value) for value in [full, both, near] + far],
    )


def respond_whole(block, pair_at, unit_count, sizes):
    wide_count, pair_count, aux_count = sizes
    local_atoms, block_size, _ = block.shape
    square = block_size * block_size
    chunk_count, _, _ = small_layout(unit_count, block_size)
    group = max(1, min(local_atoms, 16 // chunk_count))
    row_count = aux_count * 2 // pair_count
    part = pltpu.VMEM((row_count // 2, aux_count), F32)
    return pl.pallas_call(
        kernel_of(whole_kernel, wide_count, unit_count),
        out_shape=(part, part),
        in_specs=[SMEM, VMEM],
        out_specs=(VMEM, VMEM),
        scratch_shapes=[
            pltpu.VMEM((wide_count * local_atoms, square, aux_count), BF16),
            pltpu.VMEM((row_count, group * CHUNK * square), BF16),
            pltpu.VMEM((row_count, group * CHUNK * square), BF16),
        ],
        compiler_params=pltpu.CompilerParams(vmem_limit_bytes=56 * 2**20),
        name="whole",
    )(pair_at, lax.all_gather(block, "wide", axis=0, tiled=True))


def local(three_center, occ_green, virt_green, occ_column, partner_live):
    local_atoms, block_size, wide_row = three_center.shape
    aux_count = wide_row // block_size
    wide_count, pair_count = lax.axis_size("wide"), lax.axis_size("pair")
    sizes = wide_count, pair_count, aux_count
    unit_count = pair_count * occ_green.shape[1]
    _, _, lanes = small_layout(unit_count, block_size)
    wide_at = scalar(lax.axis_index("wide"))
    pair_at = scalar(lax.axis_index("pair"))
    partner = [(p, p ^ 1) for p in range(pair_count)]
    across = [(p, p ^ 2) for p in range(pair_count)]

    block, small = pl.pallas_call(
        kernel_of(pack_kernel, unit_count),
        out_shape=(
            pltpu.VMEM((local_atoms, block_size, wide_row + lanes), BF16),
            pltpu.VMEM((local_atoms, block_size, lanes), BF16),
        ),
        in_specs=[SMEM, SMEM, SMEM, VMEM, VMEM, VMEM],
        out_specs=(VMEM, VMEM),
        name="pack",
    )(pair_at, occ_column.T, partner_live.T, three_center, occ_green, virt_green)
    two = small + lax.ppermute(small, "pair", partner)
    four = two + lax.ppermute(two, "pair", across)
    early = lax.dynamic_update_slice(block, two, (0, 0, wide_row))
    full = lax.dynamic_update_slice(block, four, (0, 0, wide_row))
    if wide_count == 8 and unit_count <= 2 * CHUNK:
        keep, send = respond_direct(early, full, two, wide_at, pair_at, unit_count, sizes)
    else:
        keep, send = respond_whole(full, pair_at, unit_count, sizes)
    return keep + lax.ppermute(send, "pair", partner)


def solution(mesh):
    placed = (
        P("wide", None, None),
        P("wide", "pair", None, None),
        P("wide", "pair", None, None),
        P("wide", "pair"),
        P("wide", "pair"),
    )
    return jax.shard_map(
        local, mesh=mesh, in_specs=placed, out_specs=P("pair", None), check_vma=False
    )
```

```python
import jax
import jax.numpy as jnp
from jax import lax
from jax.experimental import pallas as pl
from jax.experimental.pallas import tpu as pltpu
from jax.sharding import PartitionSpec as P

CHUNK = 4
BASE = 256
PAIRS = ((4, 5), (6, 7), (0, 1), (2, 3))
F32, BF16 = jnp.float32, jnp.bfloat16
VMEM = pl.BlockSpec(memory_space=pltpu.VMEM)
SMEM = pl.BlockSpec(memory_space=pltpu.SMEM)


def ceil_to(value, step):
    return -(-value // step) * step


def iota(shape, axis):
    return lax.broadcasted_iota(jnp.int32, shape, axis)


def scalar(value):
    return value.astype(jnp.int32).reshape(1)


def in_vmem(value):
    return pltpu.with_memory_space_constraint(value, pltpu.VMEM)


def small_layout(unit_count, block_size):
    chunk_count = -(-unit_count // CHUNK)
    column_at = ceil_to(chunk_count * 2 * CHUNK * block_size, 128)
    return chunk_count, column_at, ceil_to(column_at + 2 * unit_count, 128)


def pack_kernel(unit_count, pair_ref, column_ref, live_ref, tc_ref, occ_ref, virt_ref, block_ref, small_ref):
    local_atoms, own_units, block_size, _ = occ_ref.shape
    wide_row = tc_ref.shape[2]
    _, column_at, lanes = small_layout(unit_count, block_size)
    row, lane = iota((block_size, lanes), 0), iota((block_size, lanes), 1)
    packed = jnp.zeros((local_atoms * block_size, lanes), F32)
    columns = [jnp.zeros((block_size, lanes), F32) for _ in range(local_atoms)]
    for slot in range(own_units):
        unit = pair_ref[0] * own_units + slot
        at = (unit // CHUNK) * (2 * CHUNK * block_size) + (unit % CHUNK) * block_size
        occ = jnp.concatenate(
            [
                occ_ref[atom, slot].astype(F32) * live_ref[slot, atom].astype(F32)
                for atom in range(local_atoms)
            ],
            axis=0,
        ).astype(BF16)
        virt = jnp.concatenate(
            [virt_ref[atom, slot].astype(F32) for atom in range(local_atoms)], axis=0
        ).astype(BF16)
        occ_place = (lane == at + row).astype(BF16)
        virt_place = (lane == at + CHUNK * block_size + row).astype(BF16)
        packed += jnp.dot(occ, occ_place, preferred_element_type=F32)
        packed += jnp.dot(virt, virt_place, preferred_element_type=F32)
        for atom in range(local_atoms):
            column = column_ref[slot, atom]
            high = column // BASE
            low = column - high * BASE
            columns[atom] += jnp.where(lane == column_at + unit, high.astype(F32), 0.0)
            columns[atom] += jnp.where(
                lane == column_at + unit_count + unit, low.astype(F32), 0.0
            )
    packed = (packed + jnp.concatenate(columns, axis=0)).astype(BF16)
    packed = packed.reshape(local_atoms, block_size, lanes)
    block_ref[:, :, :wide_row] = tc_ref[...]
    block_ref[:, :, wide_row:] = packed
    small_ref[...] = packed


def in_rows(block, aux_count):
    parts = range(block.shape[0])
    return jnp.concatenate([block[:, at * aux_count : (at + 1) * aux_count] for at in parts], axis=0)


def own_rows(rows, outer, row_count):
    found = rows[:, :row_count]
    for at in range(1, rows.shape[1] // row_count):
        found = jnp.where(outer == at, rows[:, at * row_count : (at + 1) * row_count], found)
    return found


def turned(rows):
    found = []
    for at in range(0, len(rows), 2):
        both = jnp.concatenate(rows[at : at + 2], axis=1)
        both = jnp.concatenate([both, both], axis=0).T
        found += jnp.split(both, len(rows[at : at + 2]), axis=0)
    return found


def spread_small(block_size, lane_at):
    square = block_size * block_size
    wide_unit = CHUNK * square
    row, lane = iota((128, 2 * wide_unit), 0), iota((128, 2 * wide_unit), 1)
    inner = lane % wide_unit
    unit, sigma, lam = inner // square, (inner // block_size) % block_size, inner % block_size
    within = jnp.where(lane >= wide_unit, sigma + CHUNK * block_size, lam)
    return (row == unit * block_size + within + lane_at).astype(BF16)


def contract(rows, smalls, spread, both_ref, first):
    block_size, wide_unit = smalls[0].shape[0], spread.shape[1] // 2
    wide = jnp.dot(jnp.concatenate(smalls, axis=0), spread, preferred_element_type=F32)
    for member in range(len(rows)):
        values = wide[member * block_size : (member + 1) * block_size]
        occ, virt = values[:, :wide_unit], values[:, wide_unit:]
        weights = jnp.concatenate(
            [jnp.broadcast_to(virt[nu : nu + 1], occ.shape) * occ for nu in range(block_size)], axis=0
        )
        high = weights.astype(BF16)
        low = (weights - high.astype(F32)).astype(BF16)
        at = slice(first + member * wide_unit, first + (member + 1) * wide_unit)
        both_ref[:, at] = jnp.dot(
            rows[member], jnp.concatenate([high, low], axis=0), preferred_element_type=F32
        ).astype(BF16)


def join_columns(digits, unit_count):
    row, lane = (iota((digits.shape[1], ceil_to(unit_count, 128)), axis) for axis in range(2))
    join = jnp.where(row == lane, float(BASE), 0.0) + jnp.where(row == unit_count + lane, 1.0, 0.0)
    join = jnp.where(lane < unit_count, join, 0.0).astype(BF16)
    return jnp.dot(digits, join, preferred_element_type=F32).astype(jnp.int32)


def write_rows(total, half, keep_ref, send_ref):
    row_count = keep_ref.shape[0]
    keep_ref[...] = jnp.where(half == 0, total[:row_count], total[row_count:])
    send_ref[...] = jnp.where(half == 0, total[row_count:], total[:row_count])


def kernel_of(function, *sizes):
    def kernel(*refs):
        function(*sizes, *refs)

    return kernel


def contract_kernel(unit_count, wide_ref, pair_ref, own_ref, early_ref, *refs):
    count = len(PAIRS)
    block_refs = refs[:count]
    both_ref, rows_ref, index_ref, small_ref = refs[count:]
    local_atoms, block_size, _ = own_ref.shape
    aux_count, row_count = rows_ref.shape[2], both_ref.shape[0]
    chunk_count, column_at, lanes = small_layout(unit_count, block_size)
    side, half, outer = wide_ref[0], pair_ref[0] % 2, pair_ref[0] // 2
    for slot, (even, odd) in enumerate(PAIRS):
        place = (side ^ jnp.where(half == 0, even, odd)) // 2 * local_atoms
        for atom in range(local_atoms):
            block = block_refs[slot][atom]
            if even == 0:
                block = jnp.where(half == 0, own_ref[atom], block)
            rows_ref[place + atom] = in_rows(block, aux_count)
            small = block[:, block_size * aux_count :]
            small_ref[place + atom] = early_ref[atom] if slot == 0 else small
    atoms = range(count * local_atoms)
    rows = turned([own_rows(rows_ref[atom], outer, row_count) for atom in atoms])
    for chunk in range(chunk_count):
        lane_at = chunk * 2 * CHUNK * block_size
        tile = lane_at // 128 * 128
        smalls = [small_ref[atom, :, tile : tile + 128] for atom in atoms]
        first = chunk * len(atoms) * CHUNK * block_size * block_size
        contract(rows, smalls, spread_small(block_size, lane_at - tile), both_ref, first)
    digits = jnp.concatenate([small_ref[atom, :, column_at:] for atom in atoms], axis=0)
    joined = join_columns(digits, unit_count)
    for atom in atoms:
        for unit in range(unit_count):
            index_ref[atom, unit] = joined[atom * block_size, unit]


def respond_kernel(unit_count, wide_ref, pair_ref, index_ref, own_ref, both_ref, near_ref, *refs):
    count = len(PAIRS)
    far_refs = refs[:count]
    keep_ref, send_ref, rows_ref = refs[count:]
    local_atoms, block_size, _ = own_ref.shape
    aux_count = rows_ref.shape[2]
    chunk_count, _, _ = small_layout(unit_count, block_size)
    side, half = wide_ref[0], pair_ref[0] % 2
    for slot, (even, odd) in enumerate(PAIRS):
        owner = side ^ jnp.where(half == 0, odd, even)
        for atom in range(local_atoms):
            rows_ref[owner * local_atoms + atom] = in_rows(far_refs[slot][atom], aux_count)
    for atom in range(local_atoms):
        rows_ref[side * local_atoms + atom] = in_rows(own_ref[atom], aux_count)
    for place in range(count):
        owner = place * 2 + (side ^ half) % 2
        for atom in range(local_atoms):
            rows_ref[owner * local_atoms + atom] = near_ref[place * local_atoms + atom]
    found = []
    for chunk in range(chunk_count):
        for atom in range(count * local_atoms):
            for unit in range(chunk * CHUNK, (chunk + 1) * CHUNK):
                if unit < unit_count:
                    found.append(rows_ref[index_ref[atom, unit]])
                else:
                    found.append(jnp.zeros(rows_ref.shape[1:], BF16))
    total = jnp.dot(both_ref[...], jnp.concatenate(found, axis=0), preferred_element_type=F32)
    write_rows(total, half, keep_ref, send_ref)


def whole_kernel(wide_count, unit_count, pair_ref, block_ref, *refs):
    keep_ref, send_ref, rows_ref, both_ref = refs
    atom_total, block_size, _ = block_ref.shape
    aux_count = rows_ref.shape[2]
    row_count = both_ref.shape[0]
    local_atoms = atom_total // wide_count
    chunk_count, column_at, _ = small_layout(unit_count, block_size)
    half, outer = pair_ref[0] % 2, pair_ref[0] // 2
    group = both_ref.shape[1] // (CHUNK * block_size * block_size)

    @pl.loop(0, atom_total)
    def _(atom):
        rows_ref[atom] = in_rows(block_ref[atom], aux_count)

    def work(step, total):
        positions = [step * group + member for member in range(group)]
        atoms = [(at // local_atoms * 2 + half) * local_atoms + at % local_atoms for at in positions]
        rows = turned([own_rows(rows_ref[atom], outer, row_count) for atom in atoms])
        column_tile = block_size * aux_count + column_at
        digits = jnp.concatenate([block_ref[atom, :, column_tile:] for atom in atoms], axis=0)
        joined = join_columns(digits, unit_count)
        for chunk in range(chunk_count):
            lane_at = chunk * 2 * CHUNK * block_size
            tile = block_size * aux_count + lane_at // 128 * 128
            smalls = [block_ref[atom, :, tile : tile + 128] for atom in atoms]
            contract(rows, smalls, spread_small(block_size, lane_at % 128), both_ref, 0)
            found = []
            for member in range(group):
                for unit in range(chunk * CHUNK, (chunk + 1) * CHUNK):
                    if unit < unit_count:
                        found.append(rows_ref[joined[member * block_size, unit]])
                    else:
                        found.append(jnp.zeros(rows_ref.shape[1:], BF16))
            total += jnp.dot(
                both_ref[...], jnp.concatenate(found, axis=0), preferred_element_type=F32
            )
        return total

    total = jnp.zeros((row_count, aux_count), F32)
    total = lax.fori_loop(0, atom_total // 2 // group, work, total)
    write_rows(total, half, keep_ref, send_ref)


def respond_direct(early, full, early_small, wide_at, pair_at, unit_count, sizes):
    wide_count, pair_count, aux_count = sizes
    local_atoms, block_size, _ = full.shape
    square = block_size * block_size
    partner = [(p, p ^ 1) for p in range(pair_count)]
    across = [(p, p ^ 2) for p in range(pair_count)]
    fetched, far = [], []
    for slot, (even, odd) in enumerate(PAIRS):
        route = [
            ((w ^ d) * pair_count + p, w * pair_count + p)
            for w in range(wide_count)
            for p in range(pair_count)
            for d in (odd if p % 2 else even,)
            if d
        ]
        fetched.append(lax.ppermute(full if slot else early, ("wide", "pair"), route))
        far.append(lax.ppermute(fetched[-1], "pair", partner))
    small = fetched[0][:, :, block_size * aux_count :]
    small = small + lax.ppermute(small, "pair", across)
    chunk_count, _, lanes = small_layout(unit_count, block_size)
    near_atoms = len(PAIRS) * local_atoms
    row_count = aux_count * 2 // pair_count
    width = near_atoms * chunk_count * CHUNK * square
    both, near, index = pl.pallas_call(
        kernel_of(contract_kernel, unit_count),
        out_shape=(
            pltpu.VMEM((row_count, width), BF16),
            pltpu.VMEM((near_atoms, square, aux_count), BF16),
            pltpu.SMEM((near_atoms, unit_count), jnp.int32),
        ),
        in_specs=[SMEM, SMEM] + [VMEM] * (2 + len(PAIRS)),
        out_specs=(VMEM, VMEM, SMEM),
        scratch_shapes=[pltpu.VMEM((near_atoms, block_size, lanes), BF16)],
        name="contract",
    )(wide_at, pair_at, *[in_vmem(value) for value in [full, small] + fetched])
    part = pltpu.VMEM((row_count // 2, aux_count), F32)
    return pl.pallas_call(
        kernel_of(respond_kernel, unit_count),
        out_shape=(part, part),
        in_specs=[SMEM, SMEM, SMEM] + [VMEM] * (3 + len(PAIRS)),
        out_specs=(VMEM, VMEM),
        scratch_shapes=[pltpu.VMEM((wide_count * local_atoms, square, aux_count), BF16)],
        name="respond",
    )(
        wide_at,
        pair_at,
        pltpu.with_memory_space_constraint(index, pltpu.SMEM),
        *[in_vmem(value) for value in [full, both, near] + far],
    )


def respond_whole(block, pair_at, unit_count, sizes):
    wide_count, pair_count, aux_count = sizes
    local_atoms, block_size, _ = block.shape
    square = block_size * block_size
    chunk_count, _, _ = small_layout(unit_count, block_size)
    group = max(1, min(local_atoms, 16 // chunk_count))
    row_count = aux_count * 2 // pair_count
    part = pltpu.VMEM((row_count // 2, aux_count), F32)
    return pl.pallas_call(
        kernel_of(whole_kernel, wide_count, unit_count),
        out_shape=(part, part),
        in_specs=[SMEM, VMEM],
        out_specs=(VMEM, VMEM),
        scratch_shapes=[
            pltpu.VMEM((wide_count * local_atoms, square, aux_count), BF16),
            pltpu.VMEM((row_count, group * CHUNK * square), BF16),
        ],
        compiler_params=pltpu.CompilerParams(vmem_limit_bytes=56 * 2**20),
        name="whole",
    )(pair_at, lax.all_gather(block, "wide", axis=0, tiled=True))


def local(three_center, occ_green, virt_green, occ_column, partner_live):
    local_atoms, block_size, wide_row = three_center.shape
    aux_count = wide_row // block_size
    wide_count, pair_count = lax.axis_size("wide"), lax.axis_size("pair")
    sizes = wide_count, pair_count, aux_count
    unit_count = pair_count * occ_green.shape[1]
    _, _, lanes = small_layout(unit_count, block_size)
    wide_at = scalar(lax.axis_index("wide"))
    pair_at = scalar(lax.axis_index("pair"))
    partner = [(p, p ^ 1) for p in range(pair_count)]
    across = [(p, p ^ 2) for p in range(pair_count)]

    block, small = pl.pallas_call(
        kernel_of(pack_kernel, unit_count),
        out_shape=(
            pltpu.VMEM((local_atoms, block_size, wide_row + lanes), BF16),
            pltpu.VMEM((local_atoms, block_size, lanes), BF16),
        ),
        in_specs=[SMEM, SMEM, SMEM, VMEM, VMEM, VMEM],
        out_specs=(VMEM, VMEM),
        name="pack",
    )(pair_at, occ_column.T, partner_live.T, three_center, occ_green, virt_green)
    two = small + lax.ppermute(small, "pair", partner)
    four = two + lax.ppermute(two, "pair", across)
    early = lax.dynamic_update_slice(block, two, (0, 0, wide_row))
    full = lax.dynamic_update_slice(block, four, (0, 0, wide_row))
    if wide_count == 8 and unit_count <= 2 * CHUNK:
        keep, send = respond_direct(early, full, two, wide_at, pair_at, unit_count, sizes)
    else:
        keep, send = respond_whole(full, pair_at, unit_count, sizes)
    return keep + lax.ppermute(send, "pair", partner)


def solution(mesh):
    placed = (
        P("wide", None, None),
        P("wide", "pair", None, None),
        P("wide", "pair", None, None),
        P("wide", "pair"),
        P("wide", "pair"),
    )
    return jax.shard_map(
        local, mesh=mesh, in_specs=placed, out_specs=P("pair", None), check_vma=False
    )
```

```python
import jax
import jax.numpy as jnp
from jax import lax
from jax.experimental import pallas as pl
from jax.experimental.pallas import tpu as pltpu
from jax.sharding import PartitionSpec as P

CHUNK = 4
BASE = 256
PAIRS = ((6, 7), (4, 5), (0, 1), (2, 3))
F32, BF16 = jnp.float32, jnp.bfloat16
VMEM = pl.BlockSpec(memory_space=pltpu.VMEM)
SMEM = pl.BlockSpec(memory_space=pltpu.SMEM)


def ceil_to(value, step):
    return -(-value // step) * step


def iota(shape, axis):
    return lax.broadcasted_iota(jnp.int32, shape, axis)


def scalar(value):
    return value.astype(jnp.int32).reshape(1)


def in_vmem(value):
    return pltpu.with_memory_space_constraint(value, pltpu.VMEM)


def small_layout(unit_count, block_size):
    chunk_count = -(-unit_count // CHUNK)
    column_at = ceil_to(chunk_count * 2 * CHUNK * block_size, 128)
    return chunk_count, column_at, ceil_to(column_at + 2 * unit_count, 128)


def pack_kernel(unit_count, pair_ref, column_ref, live_ref, tc_ref, occ_ref, virt_ref, block_ref, small_ref):
    local_atoms, own_units, block_size, _ = occ_ref.shape
    wide_row = tc_ref.shape[2]
    _, column_at, lanes = small_layout(unit_count, block_size)
    row, lane = iota((block_size, lanes), 0), iota((block_size, lanes), 1)
    packed = jnp.zeros((local_atoms * block_size, lanes), F32)
    columns = [jnp.zeros((block_size, lanes), F32) for _ in range(local_atoms)]
    for slot in range(own_units):
        unit = pair_ref[0] * own_units + slot
        at = (unit // CHUNK) * (2 * CHUNK * block_size) + (unit % CHUNK) * block_size
        occ = jnp.concatenate(
            [
                occ_ref[atom, slot].astype(F32) * live_ref[slot, atom].astype(F32)
                for atom in range(local_atoms)
            ],
            axis=0,
        ).astype(BF16)
        virt = jnp.concatenate(
            [virt_ref[atom, slot].astype(F32) for atom in range(local_atoms)], axis=0
        ).astype(BF16)
        occ_place = (lane == at + row).astype(BF16)
        virt_place = (lane == at + CHUNK * block_size + row).astype(BF16)
        packed += jnp.dot(occ, occ_place, preferred_element_type=F32)
        packed += jnp.dot(virt, virt_place, preferred_element_type=F32)
        for atom in range(local_atoms):
            column = column_ref[slot, atom]
            high = column // BASE
            low = column - high * BASE
            columns[atom] += jnp.where(lane == column_at + unit, high.astype(F32), 0.0)
            columns[atom] += jnp.where(
                lane == column_at + unit_count + unit, low.astype(F32), 0.0
            )
    packed = (packed + jnp.concatenate(columns, axis=0)).astype(BF16)
    packed = packed.reshape(local_atoms, block_size, lanes)
    block_ref[:, :, :wide_row] = tc_ref[...]
    block_ref[:, :, wide_row:] = packed
    small_ref[...] = packed


def in_rows(block, aux_count):
    parts = range(block.shape[0])
    return jnp.concatenate([block[:, at * aux_count : (at + 1) * aux_count] for at in parts], axis=0)


def own_rows(rows, outer, row_count):
    found = rows[:, :row_count]
    for at in range(1, rows.shape[1] // row_count):
        found = jnp.where(outer == at, rows[:, at * row_count : (at + 1) * row_count], found)
    return found


def turned(rows):
    found = []
    for at in range(0, len(rows), 2):
        both = jnp.concatenate(rows[at : at + 2], axis=1)
        both = jnp.concatenate([both, both], axis=0).T
        found += jnp.split(both, len(rows[at : at + 2]), axis=0)
    return found


def spread_small(block_size, lane_at):
    square = block_size * block_size
    wide_unit = CHUNK * square
    row, lane = iota((128, 2 * wide_unit), 0), iota((128, 2 * wide_unit), 1)
    inner = lane % wide_unit
    unit, sigma, lam = inner // square, (inner // block_size) % block_size, inner % block_size
    within = jnp.where(lane >= wide_unit, sigma + CHUNK * block_size, lam)
    return (row == unit * block_size + within + lane_at).astype(BF16)


def contract(rows, smalls, spread, both_ref, first):
    block_size, wide_unit = smalls[0].shape[0], spread.shape[1] // 2
    wide = jnp.dot(jnp.concatenate(smalls, axis=0), spread, preferred_element_type=F32)
    for member in range(len(rows)):
        values = wide[member * block_size : (member + 1) * block_size]
        occ, virt = values[:, :wide_unit], values[:, wide_unit:]
        weights = jnp.concatenate(
            [jnp.broadcast_to(virt[nu : nu + 1], occ.shape) * occ for nu in range(block_size)], axis=0
        )
        high = weights.astype(BF16)
        low = (weights - high.astype(F32)).astype(BF16)
        at = slice(first + member * wide_unit, first + (member + 1) * wide_unit)
        both_ref[:, at] = jnp.dot(
            rows[member], jnp.concatenate([high, low], axis=0), preferred_element_type=F32
        ).astype(BF16)


def join_columns(digits, unit_count):
    row, lane = (iota((digits.shape[1], ceil_to(unit_count, 128)), axis) for axis in range(2))
    join = jnp.where(row == lane, float(BASE), 0.0) + jnp.where(row == unit_count + lane, 1.0, 0.0)
    join = jnp.where(lane < unit_count, join, 0.0).astype(BF16)
    return jnp.dot(digits, join, preferred_element_type=F32).astype(jnp.int32)


def write_rows(total, half, keep_ref, send_ref):
    row_count = keep_ref.shape[0]
    keep_ref[...] = jnp.where(half == 0, total[:row_count], total[row_count:])
    send_ref[...] = jnp.where(half == 0, total[row_count:], total[:row_count])


def kernel_of(function, *sizes):
    def kernel(*refs):
        function(*sizes, *refs)

    return kernel


def contract_kernel(unit_count, wide_ref, pair_ref, own_ref, early_ref, *refs):
    count = len(PAIRS)
    block_refs = refs[:count]
    both_ref, rows_ref, index_ref, small_ref = refs[count:]
    local_atoms, block_size, _ = own_ref.shape
    aux_count, row_count = rows_ref.shape[2], both_ref.shape[0]
    chunk_count, column_at, lanes = small_layout(unit_count, block_size)
    side, half, outer = wide_ref[0], pair_ref[0] % 2, pair_ref[0] // 2
    for slot, (even, odd) in enumerate(PAIRS):
        place = (side ^ jnp.where(half == 0, even, odd)) // 2 * local_atoms
        for atom in range(local_atoms):
            block = block_refs[slot][atom]
            if even == 0:
                block = jnp.where(half == 0, own_ref[atom], block)
            rows_ref[place + atom] = in_rows(block, aux_count)
            small = block[:, block_size * aux_count :]
            small_ref[place + atom] = early_ref[atom] if slot == 0 else small
    atoms = range(count * local_atoms)
    rows = turned([own_rows(rows_ref[atom], outer, row_count) for atom in atoms])
    for chunk in range(chunk_count):
        lane_at = chunk * 2 * CHUNK * block_size
        tile = lane_at // 128 * 128
        smalls = [small_ref[atom, :, tile : tile + 128] for atom in atoms]
        first = chunk * len(atoms) * CHUNK * block_size * block_size
        contract(rows, smalls, spread_small(block_size, lane_at - tile), both_ref, first)
    digits = jnp.concatenate([small_ref[atom, :, column_at:] for atom in atoms], axis=0)
    joined = join_columns(digits, unit_count)
    for atom in atoms:
        for unit in range(unit_count):
            index_ref[atom, unit] = joined[atom * block_size, unit]


def respond_kernel(unit_count, wide_ref, pair_ref, index_ref, own_ref, both_ref, near_ref, *refs):
    count = len(PAIRS)
    far_refs = refs[:count]
    keep_ref, send_ref, rows_ref = refs[count:]
    local_atoms, block_size, _ = own_ref.shape
    aux_count = rows_ref.shape[2]
    chunk_count, _, _ = small_layout(unit_count, block_size)
    side, half = wide_ref[0], pair_ref[0] % 2
    for slot, (even, odd) in enumerate(PAIRS):
        owner = side ^ jnp.where(half == 0, odd, even)
        for atom in range(local_atoms):
            rows_ref[owner * local_atoms + atom] = in_rows(far_refs[slot][atom], aux_count)
    for atom in range(local_atoms):
        rows_ref[side * local_atoms + atom] = in_rows(own_ref[atom], aux_count)
    for place in range(count):
        owner = place * 2 + (side ^ half) % 2
        for atom in range(local_atoms):
            rows_ref[owner * local_atoms + atom] = near_ref[place * local_atoms + atom]
    found = []
    for chunk in range(chunk_count):
        for atom in range(count * local_atoms):
            for unit in range(chunk * CHUNK, (chunk + 1) * CHUNK):
                if unit < unit_count:
                    found.append(rows_ref[index_ref[atom, unit]])
                else:
                    found.append(jnp.zeros(rows_ref.shape[1:], BF16))
    total = jnp.dot(both_ref[...], jnp.concatenate(found, axis=0), preferred_element_type=F32)
    write_rows(total, half, keep_ref, send_ref)


def whole_kernel(wide_count, unit_count, pair_ref, block_ref, *refs):
    keep_ref, send_ref, rows_ref, both_ref = refs
    atom_total, block_size, _ = block_ref.shape
    aux_count = rows_ref.shape[2]
    row_count = both_ref.shape[0]
    local_atoms = atom_total // wide_count
    chunk_count, column_at, _ = small_layout(unit_count, block_size)
    half, outer = pair_ref[0] % 2, pair_ref[0] // 2
    group = both_ref.shape[1] // (CHUNK * block_size * block_size)

    @pl.loop(0, atom_total)
    def _(atom):
        rows_ref[atom] = in_rows(block_ref[atom], aux_count)

    def work(step, total):
        positions = [step * group + member for member in range(group)]
        atoms = [(at // local_atoms * 2 + half) * local_atoms + at % local_atoms for at in positions]
        rows = turned([own_rows(rows_ref[atom], outer, row_count) for atom in atoms])
        column_tile = block_size * aux_count + column_at
        digits = jnp.concatenate([block_ref[atom, :, column_tile:] for atom in atoms], axis=0)
        joined = join_columns(digits, unit_count)
        for chunk in range(chunk_count):
            lane_at = chunk * 2 * CHUNK * block_size
            tile = block_size * aux_count + lane_at // 128 * 128
            smalls = [block_ref[atom, :, tile : tile + 128] for atom in atoms]
            contract(rows, smalls, spread_small(block_size, lane_at % 128), both_ref, 0)
            found = []
            for member in range(group):
                for unit in range(chunk * CHUNK, (chunk + 1) * CHUNK):
                    if unit < unit_count:
                        found.append(rows_ref[joined[member * block_size, unit]])
                    else:
                        found.append(jnp.zeros(rows_ref.shape[1:], BF16))
            total += jnp.dot(
                both_ref[...], jnp.concatenate(found, axis=0), preferred_element_type=F32
            )
        return total

    total = jnp.zeros((row_count, aux_count), F32)
    total = lax.fori_loop(0, atom_total // 2 // group, work, total)
    write_rows(total, half, keep_ref, send_ref)


def respond_direct(early, full, early_small, wide_at, pair_at, unit_count, sizes):
    wide_count, pair_count, aux_count = sizes
    local_atoms, block_size, _ = full.shape
    square = block_size * block_size
    partner = [(p, p ^ 1) for p in range(pair_count)]
    across = [(p, p ^ 2) for p in range(pair_count)]
    fetched, far = [], []
    for slot, (even, odd) in enumerate(PAIRS):
        route = [
            ((w ^ d) * pair_count + p, w * pair_count + p)
            for w in range(wide_count)
            for p in range(pair_count)
            for d in (odd if p % 2 else even,)
            if d
        ]
        fetched.append(lax.ppermute(full if slot else early, ("wide", "pair"), route))
        far.append(lax.ppermute(fetched[-1], "pair", partner))
    small = fetched[0][:, :, block_size * aux_count :]
    small = small + lax.ppermute(small, "pair", across)
    chunk_count, _, lanes = small_layout(unit_count, block_size)
    near_atoms = len(PAIRS) * local_atoms
    row_count = aux_count * 2 // pair_count
    width = near_atoms * chunk_count * CHUNK * square
    both, near, index = pl.pallas_call(
        kernel_of(contract_kernel, unit_count),
        out_shape=(
            pltpu.VMEM((row_count, width), BF16),
            pltpu.VMEM((near_atoms, square, aux_count), BF16),
            pltpu.SMEM((near_atoms, unit_count), jnp.int32),
        ),
        in_specs=[SMEM, SMEM] + [VMEM] * (2 + len(PAIRS)),
        out_specs=(VMEM, VMEM, SMEM),
        scratch_shapes=[pltpu.VMEM((near_atoms, block_size, lanes), BF16)],
        name="contract",
    )(wide_at, pair_at, *[in_vmem(value) for value in [full, small] + fetched])
    part = pltpu.VMEM((row_count // 2, aux_count), F32)
    return pl.pallas_call(
        kernel_of(respond_kernel, unit_count),
        out_shape=(part, part),
        in_specs=[SMEM, SMEM, SMEM] + [VMEM] * (3 + len(PAIRS)),
        out_specs=(VMEM, VMEM),
        scratch_shapes=[pltpu.VMEM((wide_count * local_atoms, square, aux_count), BF16)],
        name="respond",
    )(
        wide_at,
        pair_at,
        pltpu.with_memory_space_constraint(index, pltpu.SMEM),
        *[in_vmem(value) for value in [full, both, near] + far],
    )


def respond_whole(block, pair_at, unit_count, sizes):
    wide_count, pair_count, aux_count = sizes
    local_atoms, block_size, _ = block.shape
    square = block_size * block_size
    chunk_count, _, _ = small_layout(unit_count, block_size)
    group = max(1, min(local_atoms, 16 // chunk_count))
    row_count = aux_count * 2 // pair_count
    part = pltpu.VMEM((row_count // 2, aux_count), F32)
    return pl.pallas_call(
        kernel_of(whole_kernel, wide_count, unit_count),
        out_shape=(part, part),
        in_specs=[SMEM, VMEM],
        out_specs=(VMEM, VMEM),
        scratch_shapes=[
            pltpu.VMEM((wide_count * local_atoms, square, aux_count), BF16),
            pltpu.VMEM((row_count, group * CHUNK * square), BF16),
        ],
        compiler_params=pltpu.CompilerParams(vmem_limit_bytes=56 * 2**20),
        name="whole",
    )(pair_at, lax.all_gather(block, "wide", axis=0, tiled=True))


def local(three_center, occ_green, virt_green, occ_column, partner_live):
    local_atoms, block_size, wide_row = three_center.shape
    aux_count = wide_row // block_size
    wide_count, pair_count = lax.axis_size("wide"), lax.axis_size("pair")
    sizes = wide_count, pair_count, aux_count
    unit_count = pair_count * occ_green.shape[1]
    _, _, lanes = small_layout(unit_count, block_size)
    wide_at = scalar(lax.axis_index("wide"))
    pair_at = scalar(lax.axis_index("pair"))
    partner = [(p, p ^ 1) for p in range(pair_count)]
    across = [(p, p ^ 2) for p in range(pair_count)]

    block, small = pl.pallas_call(
        kernel_of(pack_kernel, unit_count),
        out_shape=(
            pltpu.VMEM((local_atoms, block_size, wide_row + lanes), BF16),
            pltpu.VMEM((local_atoms, block_size, lanes), BF16),
        ),
        in_specs=[SMEM, SMEM, SMEM, VMEM, VMEM, VMEM],
        out_specs=(VMEM, VMEM),
        name="pack",
    )(pair_at, occ_column.T, partner_live.T, three_center, occ_green, virt_green)
    two = small + lax.ppermute(small, "pair", partner)
    four = two + lax.ppermute(two, "pair", across)
    early = lax.dynamic_update_slice(block, two, (0, 0, wide_row))
    full = lax.dynamic_update_slice(block, four, (0, 0, wide_row))
    if wide_count == 8 and unit_count <= 2 * CHUNK:
        keep, send = respond_direct(early, full, two, wide_at, pair_at, unit_count, sizes)
    else:
        keep, send = respond_whole(full, pair_at, unit_count, sizes)
    return keep + lax.ppermute(send, "pair", partner)


def solution(mesh):
    placed = (
        P("wide", None, None),
        P("wide", "pair", None, None),
        P("wide", "pair", None, None),
        P("wide", "pair"),
        P("wide", "pair"),
    )
    return jax.shard_map(
        local, mesh=mesh, in_specs=placed, out_specs=P("pair", None), check_vma=False
    )
```

```python
import jax
import jax.numpy as jnp
from jax import lax
from jax.experimental import pallas as pl
from jax.experimental.pallas import tpu as pltpu
from jax.sharding import PartitionSpec as P

CHUNK = 4
BASE = 256
PAIR_STEP = 4096
PAIRS = ((6, 7), (4, 5), (0, 1), (2, 3))
F32, BF16 = jnp.float32, jnp.bfloat16
VMEM = pl.BlockSpec(memory_space=pltpu.VMEM)
SMEM = pl.BlockSpec(memory_space=pltpu.SMEM)


def ceil_to(value, step):
    return -(-value // step) * step


def iota(shape, axis):
    return lax.broadcasted_iota(jnp.int32, shape, axis)


def scalar(value):
    return value.astype(jnp.int32).reshape(1)


def in_vmem(value):
    return pltpu.with_memory_space_constraint(value, pltpu.VMEM)


def small_layout(unit_count, block_size):
    chunk_count = -(-unit_count // CHUNK)
    column_at = ceil_to(chunk_count * 2 * CHUNK * block_size, 128)
    return chunk_count, column_at, ceil_to(column_at + 2 * unit_count, 128)


def pack_kernel(unit_count, pair_ref, column_ref, live_ref, tc_ref, occ_ref, virt_ref, block_ref, small_ref):
    local_atoms, own_units, block_size, _ = occ_ref.shape
    wide_row = tc_ref.shape[2]
    _, column_at, lanes = small_layout(unit_count, block_size)
    row, lane = iota((block_size, lanes), 0), iota((block_size, lanes), 1)
    packed = jnp.zeros((local_atoms * block_size, lanes), F32)
    columns = [jnp.zeros((block_size, lanes), F32) for _ in range(local_atoms)]
    for slot in range(own_units):
        unit = pair_ref[0] * own_units + slot
        at = (unit // CHUNK) * (2 * CHUNK * block_size) + (unit % CHUNK) * block_size
        occ = jnp.concatenate(
            [
                occ_ref[atom, slot].astype(F32) * live_ref[slot, atom].astype(F32)
                for atom in range(local_atoms)
            ],
            axis=0,
        ).astype(BF16)
        virt = jnp.concatenate(
            [virt_ref[atom, slot].astype(F32) for atom in range(local_atoms)], axis=0
        ).astype(BF16)
        occ_place = (lane == at + row).astype(BF16)
        virt_place = (lane == at + CHUNK * block_size + row).astype(BF16)
        packed += jnp.dot(occ, occ_place, preferred_element_type=F32)
        packed += jnp.dot(virt, virt_place, preferred_element_type=F32)
        for atom in range(local_atoms):
            column = column_ref[slot, atom]
            high = column // BASE
            low = column - high * BASE
            columns[atom] += jnp.where(lane == column_at + unit, high.astype(F32), 0.0)
            columns[atom] += jnp.where(
                lane == column_at + unit_count + unit, low.astype(F32), 0.0
            )
    packed = (packed + jnp.concatenate(columns, axis=0)).astype(BF16)
    packed = packed.reshape(local_atoms, block_size, lanes)
    block_ref[:, :, :wide_row] = tc_ref[...]
    block_ref[:, :, wide_row:] = packed
    small_ref[...] = packed


def in_rows(block, aux_count):
    parts = range(block.shape[0])
    return jnp.concatenate([block[:, at * aux_count : (at + 1) * aux_count] for at in parts], axis=0)


def own_rows(rows, outer, row_count):
    found = rows[:, :row_count]
    for at in range(1, rows.shape[1] // row_count):
        found = jnp.where(outer == at, rows[:, at * row_count : (at + 1) * row_count], found)
    return found


def turned(rows):
    found = []
    for at in range(0, len(rows), 2):
        both = jnp.concatenate(rows[at : at + 2], axis=1)
        both = jnp.concatenate([both, both], axis=0).T
        found += jnp.split(both, len(rows[at : at + 2]), axis=0)
    return found


def spread_small(block_size, lane_at):
    square = block_size * block_size
    wide_unit = CHUNK * square
    row, lane = iota((128, 2 * wide_unit), 0), iota((128, 2 * wide_unit), 1)
    inner = lane % wide_unit
    unit, sigma, lam = inner // square, (inner // block_size) % block_size, inner % block_size
    within = jnp.where(lane >= wide_unit, sigma + CHUNK * block_size, lam)
    return (row == unit * block_size + within + lane_at).astype(BF16)


def contract(rows, smalls, spread, both_ref, first):
    block_size, wide_unit = smalls[0].shape[0], spread.shape[1] // 2
    wide = jnp.dot(jnp.concatenate(smalls, axis=0), spread, preferred_element_type=F32)
    for member in range(len(rows)):
        values = wide[member * block_size : (member + 1) * block_size]
        occ, virt = values[:, :wide_unit], values[:, wide_unit:]
        weights = jnp.concatenate(
            [jnp.broadcast_to(virt[nu : nu + 1], occ.shape) * occ for nu in range(block_size)], axis=0
        )
        high = weights.astype(BF16)
        low = (weights - high.astype(F32)).astype(BF16)
        at = slice(first + member * wide_unit, first + (member + 1) * wide_unit)
        both_ref[:, at] = jnp.dot(
            rows[member], jnp.concatenate([high, low], axis=0), preferred_element_type=F32
        ).astype(BF16)


def join_columns(digits, unit_count):
    row, lane = (iota((digits.shape[1], ceil_to(unit_count, 128)), axis) for axis in range(2))
    join = jnp.zeros(row.shape, F32)
    for member, step in enumerate((1.0, float(PAIR_STEP))):
        join += jnp.where(row == 2 * lane + member, BASE * step, 0.0)
        join += jnp.where(row == unit_count + 2 * lane + member, step, 0.0)
    join = jnp.where(lane < unit_count // 2, join, 0.0).astype(BF16)
    return jnp.dot(digits, join, preferred_element_type=F32).astype(jnp.int32)


def column_pair(joined, row, pair):
    value = joined[row, pair]
    return value & (PAIR_STEP - 1), value >> PAIR_STEP.bit_length() - 1


def write_rows(total, half, keep_ref, send_ref):
    row_count = keep_ref.shape[0]
    keep_ref[...] = jnp.where(half == 0, total[:row_count], total[row_count:])
    send_ref[...] = jnp.where(half == 0, total[row_count:], total[:row_count])


def kernel_of(function, *sizes):
    def kernel(*refs):
        function(*sizes, *refs)

    return kernel


def contract_kernel(unit_count, wide_ref, pair_ref, own_ref, early_ref, *refs):
    count = len(PAIRS)
    block_refs = refs[:count]
    both_ref, rows_ref, index_ref, small_ref = refs[count:]
    local_atoms, block_size, _ = own_ref.shape
    aux_count, row_count = rows_ref.shape[2], both_ref.shape[0]
    chunk_count, column_at, lanes = small_layout(unit_count, block_size)
    side, half, outer = wide_ref[0], pair_ref[0] % 2, pair_ref[0] // 2
    for slot, (even, odd) in enumerate(PAIRS):
        place = (side ^ jnp.where(half == 0, even, odd)) // 2 * local_atoms
        for atom in range(local_atoms):
            block = block_refs[slot][atom]
            if even == 0:
                block = jnp.where(half == 0, own_ref[atom], block)
            rows_ref[place + atom] = in_rows(block, aux_count)
            small = block[:, block_size * aux_count :]
            small_ref[place + atom] = early_ref[atom] if slot == 0 else small
    atoms = range(count * local_atoms)
    digits = jnp.concatenate([small_ref[atom, :, column_at:] for atom in atoms], axis=0)
    joined = join_columns(digits, unit_count)
    for atom in atoms:
        for pair in range(unit_count // 2):
            columns = column_pair(joined, atom * block_size, pair)
            index_ref[atom, 2 * pair], index_ref[atom, 2 * pair + 1] = columns
    rows = turned([own_rows(rows_ref[atom], outer, row_count) for atom in atoms])
    for chunk in range(chunk_count):
        lane_at = chunk * 2 * CHUNK * block_size
        tile = lane_at // 128 * 128
        smalls = [small_ref[atom, :, tile : tile + 128] for atom in atoms]
        first = chunk * len(atoms) * CHUNK * block_size * block_size
        contract(rows, smalls, spread_small(block_size, lane_at - tile), both_ref, first)


def respond_kernel(unit_count, wide_ref, pair_ref, index_ref, own_ref, both_ref, near_ref, *refs):
    count = len(PAIRS)
    far_refs = refs[:count]
    keep_ref, send_ref, rows_ref = refs[count:]
    local_atoms, block_size, _ = own_ref.shape
    aux_count = rows_ref.shape[2]
    chunk_count, _, _ = small_layout(unit_count, block_size)
    side, half = wide_ref[0], pair_ref[0] % 2
    for slot, (even, odd) in enumerate(PAIRS):
        owner = side ^ jnp.where(half == 0, odd, even)
        for atom in range(local_atoms):
            rows_ref[owner * local_atoms + atom] = in_rows(far_refs[slot][atom], aux_count)
    for atom in range(local_atoms):
        rows_ref[side * local_atoms + atom] = in_rows(own_ref[atom], aux_count)
    for place in range(count):
        owner = place * 2 + (side ^ half) % 2
        for atom in range(local_atoms):
            rows_ref[owner * local_atoms + atom] = near_ref[place * local_atoms + atom]
    found = []
    for chunk in range(chunk_count):
        for atom in range(count * local_atoms):
            for unit in range(chunk * CHUNK, (chunk + 1) * CHUNK):
                if unit < unit_count:
                    found.append(rows_ref[index_ref[atom, unit]])
                else:
                    found.append(jnp.zeros(rows_ref.shape[1:], BF16))
    total = jnp.dot(both_ref[...], jnp.concatenate(found, axis=0), preferred_element_type=F32)
    write_rows(total, half, keep_ref, send_ref)


def whole_kernel(wide_count, unit_count, pair_ref, block_ref, *refs):
    keep_ref, send_ref, rows_ref, both_ref = refs
    atom_total, block_size, _ = block_ref.shape
    aux_count = rows_ref.shape[2]
    row_count = both_ref.shape[0]
    local_atoms = atom_total // wide_count
    chunk_count, column_at, _ = small_layout(unit_count, block_size)
    half, outer = pair_ref[0] % 2, pair_ref[0] // 2
    group = both_ref.shape[1] // (CHUNK * block_size * block_size)

    @pl.loop(0, atom_total)
    def _(atom):
        rows_ref[atom] = in_rows(block_ref[atom], aux_count)

    def work(step, total):
        positions = [step * group + member for member in range(group)]
        atoms = [(at // local_atoms * 2 + half) * local_atoms + at % local_atoms for at in positions]
        rows = turned([own_rows(rows_ref[atom], outer, row_count) for atom in atoms])
        column_tile = block_size * aux_count + column_at
        digits = jnp.concatenate([block_ref[atom, :, column_tile:] for atom in atoms], axis=0)
        joined = join_columns(digits, unit_count)
        for chunk in range(chunk_count):
            lane_at = chunk * 2 * CHUNK * block_size
            tile = block_size * aux_count + lane_at // 128 * 128
            smalls = [block_ref[atom, :, tile : tile + 128] for atom in atoms]
            contract(rows, smalls, spread_small(block_size, lane_at % 128), both_ref, 0)
            found = []
            for member in range(group):
                for unit in range(chunk * CHUNK, (chunk + 1) * CHUNK):
                    if unit < unit_count:
                        columns = column_pair(joined, member * block_size, unit // 2)
                        found.append(rows_ref[columns[unit % 2]])
                    else:
                        found.append(jnp.zeros(rows_ref.shape[1:], BF16))
            total += jnp.dot(
                both_ref[...], jnp.concatenate(found, axis=0), preferred_element_type=F32
            )
        return total

    total = jnp.zeros((row_count, aux_count), F32)
    total = lax.fori_loop(0, atom_total // 2 // group, work, total)
    write_rows(total, half, keep_ref, send_ref)


def respond_direct(early, full, early_small, wide_at, pair_at, unit_count, sizes):
    wide_count, pair_count, aux_count = sizes
    local_atoms, block_size, _ = full.shape
    square = block_size * block_size
    partner = [(p, p ^ 1) for p in range(pair_count)]
    across = [(p, p ^ 2) for p in range(pair_count)]
    fetched, far = [], []
    for slot, (even, odd) in enumerate(PAIRS):
        route = [
            ((w ^ d) * pair_count + p, w * pair_count + p)
            for w in range(wide_count)
            for p in range(pair_count)
            for d in (odd if p % 2 else even,)
            if d
        ]
        fetched.append(lax.ppermute(full if slot else early, ("wide", "pair"), route))
        far.append(lax.ppermute(fetched[-1], "pair", partner))
    small = fetched[0][:, :, block_size * aux_count :]
    small = small + lax.ppermute(small, "pair", across)
    chunk_count, _, lanes = small_layout(unit_count, block_size)
    near_atoms = len(PAIRS) * local_atoms
    row_count = aux_count * 2 // pair_count
    width = near_atoms * chunk_count * CHUNK * square
    both, near, index = pl.pallas_call(
        kernel_of(contract_kernel, unit_count),
        out_shape=(
            pltpu.VMEM((row_count, width), BF16),
            pltpu.VMEM((near_atoms, square, aux_count), BF16),
            pltpu.SMEM((near_atoms, unit_count), jnp.int32),
        ),
        in_specs=[SMEM, SMEM] + [VMEM] * (2 + len(PAIRS)),
        out_specs=(VMEM, VMEM, SMEM),
        scratch_shapes=[pltpu.VMEM((near_atoms, block_size, lanes), BF16)],
        name="contract",
    )(wide_at, pair_at, *[in_vmem(value) for value in [full, small] + fetched])
    part = pltpu.VMEM((row_count // 2, aux_count), F32)
    return pl.pallas_call(
        kernel_of(respond_kernel, unit_count),
        out_shape=(part, part),
        in_specs=[SMEM, SMEM, SMEM] + [VMEM] * (3 + len(PAIRS)),
        out_specs=(VMEM, VMEM),
        scratch_shapes=[pltpu.VMEM((wide_count * local_atoms, square, aux_count), BF16)],
        name="respond",
    )(
        wide_at,
        pair_at,
        pltpu.with_memory_space_constraint(index, pltpu.SMEM),
        *[in_vmem(value) for value in [full, both, near] + far],
    )


def respond_whole(block, pair_at, unit_count, sizes):
    wide_count, pair_count, aux_count = sizes
    local_atoms, block_size, _ = block.shape
    square = block_size * block_size
    chunk_count, _, _ = small_layout(unit_count, block_size)
    group = max(1, min(local_atoms, 16 // chunk_count))
    row_count = aux_count * 2 // pair_count
    part = pltpu.VMEM((row_count // 2, aux_count), F32)
    return pl.pallas_call(
        kernel_of(whole_kernel, wide_count, unit_count),
        out_shape=(part, part),
        in_specs=[SMEM, VMEM],
        out_specs=(VMEM, VMEM),
        scratch_shapes=[
            pltpu.VMEM((wide_count * local_atoms, square, aux_count), BF16),
            pltpu.VMEM((row_count, group * CHUNK * square), BF16),
        ],
        compiler_params=pltpu.CompilerParams(vmem_limit_bytes=56 * 2**20),
        name="whole",
    )(pair_at, lax.all_gather(block, "wide", axis=0, tiled=True))


def local(three_center, occ_green, virt_green, occ_column, partner_live):
    local_atoms, block_size, wide_row = three_center.shape
    aux_count = wide_row // block_size
    wide_count, pair_count = lax.axis_size("wide"), lax.axis_size("pair")
    sizes = wide_count, pair_count, aux_count
    unit_count = pair_count * occ_green.shape[1]
    _, _, lanes = small_layout(unit_count, block_size)
    wide_at = scalar(lax.axis_index("wide"))
    pair_at = scalar(lax.axis_index("pair"))
    partner = [(p, p ^ 1) for p in range(pair_count)]
    across = [(p, p ^ 2) for p in range(pair_count)]

    block, small = pl.pallas_call(
        kernel_of(pack_kernel, unit_count),
        out_shape=(
            pltpu.VMEM((local_atoms, block_size, wide_row + lanes), BF16),
            pltpu.VMEM((local_atoms, block_size, lanes), BF16),
        ),
        in_specs=[SMEM, SMEM, SMEM, VMEM, VMEM, VMEM],
        out_specs=(VMEM, VMEM),
        name="pack",
    )(pair_at, occ_column.T, partner_live.T, three_center, occ_green, virt_green)
    two = small + lax.ppermute(small, "pair", partner)
    four = two + lax.ppermute(two, "pair", across)
    early = lax.dynamic_update_slice(block, two, (0, 0, wide_row))
    full = lax.dynamic_update_slice(block, four, (0, 0, wide_row))
    if wide_count == 8 and unit_count <= 2 * CHUNK:
        keep, send = respond_direct(early, full, two, wide_at, pair_at, unit_count, sizes)
    else:
        keep, send = respond_whole(full, pair_at, unit_count, sizes)
    return keep + lax.ppermute(send, "pair", partner)


def solution(mesh):
    placed = (
        P("wide", None, None),
        P("wide", "pair", None, None),
        P("wide", "pair", None, None),
        P("wide", "pair"),
        P("wide", "pair"),
    )
    return jax.shard_map(
        local, mesh=mesh, in_specs=placed, out_specs=P("pair", None), check_vma=False
    )
```

```python
import jax
import jax.numpy as jnp
from jax import lax
from jax.experimental import pallas as pl
from jax.experimental.pallas import tpu as pltpu
from jax.sharding import PartitionSpec as P

CHUNK = 4
BASE = 256
PAIR_STEP = 4096
PAIRS = ((6, 7), (4, 5), (0, 1), (2, 3))
F32, BF16 = jnp.float32, jnp.bfloat16
VMEM = pl.BlockSpec(memory_space=pltpu.VMEM)
SMEM = pl.BlockSpec(memory_space=pltpu.SMEM)


def ceil_to(value, step):
    return -(-value // step) * step


def iota(shape, axis):
    return lax.broadcasted_iota(jnp.int32, shape, axis)


def scalar(value):
    return value.astype(jnp.int32).reshape(1)


def in_vmem(value):
    return pltpu.with_memory_space_constraint(value, pltpu.VMEM)


def small_layout(unit_count, block_size):
    chunk_count = -(-unit_count // CHUNK)
    column_at = ceil_to(chunk_count * 2 * CHUNK * block_size, 128)
    return chunk_count, column_at, ceil_to(column_at + 2 * unit_count, 128)


def pack_kernel(unit_count, pair_ref, column_ref, live_ref, tc_ref, occ_ref, virt_ref, block_ref, small_ref):
    local_atoms, own_units, block_size, _ = occ_ref.shape
    wide_row = tc_ref.shape[2]
    _, column_at, lanes = small_layout(unit_count, block_size)
    row, lane = iota((block_size, lanes), 0), iota((block_size, lanes), 1)
    packed = jnp.zeros((local_atoms * block_size, lanes), F32)
    columns = [jnp.zeros((block_size, lanes), F32) for _ in range(local_atoms)]
    for slot in range(own_units):
        unit = pair_ref[0] * own_units + slot
        at = (unit // CHUNK) * (2 * CHUNK * block_size) + (unit % CHUNK) * block_size
        occ = jnp.concatenate(
            [
                occ_ref[atom, slot].astype(F32) * live_ref[slot, atom].astype(F32)
                for atom in range(local_atoms)
            ],
            axis=0,
        ).astype(BF16)
        virt = jnp.concatenate(
            [virt_ref[atom, slot].astype(F32) for atom in range(local_atoms)], axis=0
        ).astype(BF16)
        occ_place = (lane == at + row).astype(BF16)
        virt_place = (lane == at + CHUNK * block_size + row).astype(BF16)
        packed += jnp.dot(occ, occ_place, preferred_element_type=F32)
        packed += jnp.dot(virt, virt_place, preferred_element_type=F32)
        for atom in range(local_atoms):
            column = column_ref[slot, atom]
            high = column // BASE
            low = column - high * BASE
            columns[atom] += jnp.where(lane == column_at + unit, high.astype(F32), 0.0)
            columns[atom] += jnp.where(
                lane == column_at + unit_count + unit, low.astype(F32), 0.0
            )
    packed = (packed + jnp.concatenate(columns, axis=0)).astype(BF16)
    packed = packed.reshape(local_atoms, block_size, lanes)
    block_ref[:, :, :wide_row] = tc_ref[...]
    block_ref[:, :, wide_row:] = packed
    small_ref[...] = packed


def in_rows(block, aux_count):
    parts = range(block.shape[0])
    return jnp.concatenate([block[:, at * aux_count : (at + 1) * aux_count] for at in parts], axis=0)


def own_rows(rows, outer, row_count):
    found = rows[:, :row_count]
    for at in range(1, rows.shape[1] // row_count):
        found = jnp.where(outer == at, rows[:, at * row_count : (at + 1) * row_count], found)
    return found


def turned(rows):
    found = []
    for at in range(0, len(rows), 2):
        both = jnp.concatenate(rows[at : at + 2], axis=1)
        both = jnp.concatenate([both, both], axis=0).T
        found += jnp.split(both, len(rows[at : at + 2]), axis=0)
    return found


def spread_small(block_size, lane_at):
    square = block_size * block_size
    wide_unit = CHUNK * square
    row, lane = iota((128, 2 * wide_unit), 0), iota((128, 2 * wide_unit), 1)
    inner = lane % wide_unit
    unit, sigma, lam = inner // square, (inner // block_size) % block_size, inner % block_size
    within = jnp.where(lane >= wide_unit, sigma + CHUNK * block_size, lam)
    return (row == unit * block_size + within + lane_at).astype(BF16)


def contract(rows, smalls, spread, both_ref, first):
    block_size, wide_unit = smalls[0].shape[0], spread.shape[1] // 2
    wide = jnp.dot(jnp.concatenate(smalls, axis=0), spread, preferred_element_type=F32)
    for member in range(len(rows)):
        values = wide[member * block_size : (member + 1) * block_size]
        occ, virt = values[:, :wide_unit], values[:, wide_unit:]
        weights = jnp.concatenate(
            [jnp.broadcast_to(virt[nu : nu + 1], occ.shape) * occ for nu in range(block_size)], axis=0
        )
        high = weights.astype(BF16)
        low = (weights - high.astype(F32)).astype(BF16)
        at = slice(first + member * wide_unit, first + (member + 1) * wide_unit)
        both_ref[:, at] = jnp.dot(
            rows[member], jnp.concatenate([high, low], axis=0), preferred_element_type=F32
        ).astype(BF16)


def join_columns(digits, unit_count):
    row, lane = (iota((digits.shape[1], ceil_to(unit_count, 128)), axis) for axis in range(2))
    join = jnp.zeros(row.shape, F32)
    for member, step in enumerate((1.0, float(PAIR_STEP))):
        join += jnp.where(row == 2 * lane + member, BASE * step, 0.0)
        join += jnp.where(row == unit_count + 2 * lane + member, step, 0.0)
    join = jnp.where(lane < unit_count // 2, join, 0.0).astype(BF16)
    return jnp.dot(digits, join, preferred_element_type=F32).astype(jnp.int32)


def column_pair(joined, row, pair):
    value = joined[row, pair]
    return value & (PAIR_STEP - 1), value >> PAIR_STEP.bit_length() - 1


def write_rows(total, half, keep_ref, send_ref):
    row_count = keep_ref.shape[0]
    keep_ref[...] = jnp.where(half == 0, total[:row_count], total[row_count:])
    send_ref[...] = jnp.where(half == 0, total[row_count:], total[:row_count])


def kernel_of(function, *sizes):
    def kernel(*refs):
        function(*sizes, *refs)

    return kernel


def contract_kernel(unit_count, wide_ref, pair_ref, own_ref, early_ref, *refs):
    count = len(PAIRS)
    block_refs = refs[:count]
    both_ref, rows_ref, index_ref, small_ref = refs[count:]
    local_atoms, block_size, _ = own_ref.shape
    aux_count, row_count = rows_ref.shape[2], both_ref.shape[0]
    chunk_count, column_at, lanes = small_layout(unit_count, block_size)
    side, half, outer = wide_ref[0], pair_ref[0] % 2, pair_ref[0] // 2
    for slot, (even, odd) in enumerate(PAIRS):
        place = (side ^ jnp.where(half == 0, even, odd)) // 2 * local_atoms
        for atom in range(local_atoms):
            block = block_refs[slot][atom]
            if even == 0:
                block = jnp.where(half == 0, own_ref[atom], block)
            rows_ref[place + atom] = in_rows(block, aux_count)
            small = block[:, block_size * aux_count :]
            small_ref[place + atom] = early_ref[atom] if slot == 0 else small
    atoms = range(count * local_atoms)
    digits = jnp.concatenate([small_ref[atom, :, column_at:] for atom in atoms], axis=0)
    joined = join_columns(digits, unit_count)
    for atom in atoms:
        for pair in range(unit_count // 2):
            columns = column_pair(joined, atom * block_size, pair)
            index_ref[atom, 2 * pair], index_ref[atom, 2 * pair + 1] = columns
    rows = turned([own_rows(rows_ref[atom], outer, row_count) for atom in atoms])
    for chunk in range(chunk_count):
        lane_at = chunk * 2 * CHUNK * block_size
        tile = lane_at // 128 * 128
        smalls = [small_ref[atom, :, tile : tile + 128] for atom in atoms]
        first = chunk * len(atoms) * CHUNK * block_size * block_size
        contract(rows, smalls, spread_small(block_size, lane_at - tile), both_ref, first)


def respond_kernel(unit_count, wide_ref, pair_ref, index_ref, own_ref, both_ref, near_ref, *refs):
    count = len(PAIRS)
    far_refs = refs[:count]
    keep_ref, send_ref, rows_ref = refs[count:]
    local_atoms, block_size, _ = own_ref.shape
    aux_count = rows_ref.shape[2]
    chunk_count, _, _ = small_layout(unit_count, block_size)
    side, half = wide_ref[0], pair_ref[0] % 2
    for slot, (even, odd) in enumerate(PAIRS):
        owner = side ^ jnp.where(half == 0, odd, even)
        for atom in range(local_atoms):
            rows_ref[owner * local_atoms + atom] = in_rows(far_refs[slot][atom], aux_count)
    for atom in range(local_atoms):
        rows_ref[side * local_atoms + atom] = in_rows(own_ref[atom], aux_count)
    for place in range(count):
        owner = place * 2 + (side ^ half) % 2
        for atom in range(local_atoms):
            rows_ref[owner * local_atoms + atom] = near_ref[place * local_atoms + atom]
    total = jnp.zeros((both_ref.shape[0], aux_count), F32)
    depth = CHUNK * block_size * block_size
    for chunk in range(chunk_count):
        for atom in range(count * local_atoms):
            found = []
            for unit in range(chunk * CHUNK, (chunk + 1) * CHUNK):
                if unit < unit_count:
                    found.append(rows_ref[index_ref[atom, unit]])
                else:
                    found.append(jnp.zeros(rows_ref.shape[1:], BF16))
            at = (chunk * count * local_atoms + atom) * depth
            total += jnp.dot(
                both_ref[:, at : at + depth],
                jnp.concatenate(found, axis=0),
                preferred_element_type=F32,
            )
    write_rows(total, half, keep_ref, send_ref)


def whole_kernel(wide_count, unit_count, pair_ref, block_ref, *refs):
    keep_ref, send_ref, rows_ref, both_ref = refs
    atom_total, block_size, _ = block_ref.shape
    aux_count = rows_ref.shape[2]
    row_count = both_ref.shape[0]
    local_atoms = atom_total // wide_count
    chunk_count, column_at, _ = small_layout(unit_count, block_size)
    half, outer = pair_ref[0] % 2, pair_ref[0] // 2
    group = both_ref.shape[1] // (CHUNK * block_size * block_size)

    @pl.loop(0, atom_total)
    def _(atom):
        rows_ref[atom] = in_rows(block_ref[atom], aux_count)

    def work(step, total):
        positions = [step * group + member for member in range(group)]
        atoms = [(at // local_atoms * 2 + half) * local_atoms + at % local_atoms for at in positions]
        rows = turned([own_rows(rows_ref[atom], outer, row_count) for atom in atoms])
        column_tile = block_size * aux_count + column_at
        digits = jnp.concatenate([block_ref[atom, :, column_tile:] for atom in atoms], axis=0)
        joined = join_columns(digits, unit_count)
        for chunk in range(chunk_count):
            lane_at = chunk * 2 * CHUNK * block_size
            tile = block_size * aux_count + lane_at // 128 * 128
            smalls = [block_ref[atom, :, tile : tile + 128] for atom in atoms]
            contract(rows, smalls, spread_small(block_size, lane_at % 128), both_ref, 0)
            found = []
            for member in range(group):
                for unit in range(chunk * CHUNK, (chunk + 1) * CHUNK):
                    if unit < unit_count:
                        columns = column_pair(joined, member * block_size, unit // 2)
                        found.append(rows_ref[columns[unit % 2]])
                    else:
                        found.append(jnp.zeros(rows_ref.shape[1:], BF16))
            total += jnp.dot(
                both_ref[...], jnp.concatenate(found, axis=0), preferred_element_type=F32
            )
        return total

    total = jnp.zeros((row_count, aux_count), F32)
    total = lax.fori_loop(0, atom_total // 2 // group, work, total)
    write_rows(total, half, keep_ref, send_ref)


def respond_direct(early, full, early_small, wide_at, pair_at, unit_count, sizes):
    wide_count, pair_count, aux_count = sizes
    local_atoms, block_size, _ = full.shape
    square = block_size * block_size
    partner = [(p, p ^ 1) for p in range(pair_count)]
    across = [(p, p ^ 2) for p in range(pair_count)]
    fetched, far = [], []
    for slot, (even, odd) in enumerate(PAIRS):
        route = [
            ((w ^ d) * pair_count + p, w * pair_count + p)
            for w in range(wide_count)
            for p in range(pair_count)
            for d in (odd if p % 2 else even,)
            if d
        ]
        fetched.append(lax.ppermute(full if slot else early, ("wide", "pair"), route))
        far.append(lax.ppermute(fetched[-1], "pair", partner))
    small = fetched[0][:, :, block_size * aux_count :]
    small = small + lax.ppermute(small, "pair", across)
    chunk_count, _, lanes = small_layout(unit_count, block_size)
    near_atoms = len(PAIRS) * local_atoms
    row_count = aux_count * 2 // pair_count
    width = near_atoms * chunk_count * CHUNK * square
    both, near, index = pl.pallas_call(
        kernel_of(contract_kernel, unit_count),
        out_shape=(
            pltpu.VMEM((row_count, width), BF16),
            pltpu.VMEM((near_atoms, square, aux_count), BF16),
            pltpu.SMEM((near_atoms, unit_count), jnp.int32),
        ),
        in_specs=[SMEM, SMEM] + [VMEM] * (2 + len(PAIRS)),
        out_specs=(VMEM, VMEM, SMEM),
        scratch_shapes=[pltpu.VMEM((near_atoms, block_size, lanes), BF16)],
        name="contract",
    )(wide_at, pair_at, *[in_vmem(value) for value in [full, small] + fetched])
    part = pltpu.VMEM((row_count // 2, aux_count), F32)
    return pl.pallas_call(
        kernel_of(respond_kernel, unit_count),
        out_shape=(part, part),
        in_specs=[SMEM, SMEM, SMEM] + [VMEM] * (3 + len(PAIRS)),
        out_specs=(VMEM, VMEM),
        scratch_shapes=[pltpu.VMEM((wide_count * local_atoms, square, aux_count), BF16)],
        name="respond",
    )(
        wide_at,
        pair_at,
        pltpu.with_memory_space_constraint(index, pltpu.SMEM),
        *[in_vmem(value) for value in [full, both, near] + far],
    )


def respond_whole(block, pair_at, unit_count, sizes):
    wide_count, pair_count, aux_count = sizes
    local_atoms, block_size, _ = block.shape
    square = block_size * block_size
    chunk_count, _, _ = small_layout(unit_count, block_size)
    group = max(1, min(local_atoms, 16 // chunk_count))
    row_count = aux_count * 2 // pair_count
    part = pltpu.VMEM((row_count // 2, aux_count), F32)
    return pl.pallas_call(
        kernel_of(whole_kernel, wide_count, unit_count),
        out_shape=(part, part),
        in_specs=[SMEM, VMEM],
        out_specs=(VMEM, VMEM),
        scratch_shapes=[
            pltpu.VMEM((wide_count * local_atoms, square, aux_count), BF16),
            pltpu.VMEM((row_count, group * CHUNK * square), BF16),
        ],
        compiler_params=pltpu.CompilerParams(vmem_limit_bytes=56 * 2**20),
        name="whole",
    )(pair_at, lax.all_gather(block, "wide", axis=0, tiled=True))


def local(three_center, occ_green, virt_green, occ_column, partner_live):
    local_atoms, block_size, wide_row = three_center.shape
    aux_count = wide_row // block_size
    wide_count, pair_count = lax.axis_size("wide"), lax.axis_size("pair")
    sizes = wide_count, pair_count, aux_count
    unit_count = pair_count * occ_green.shape[1]
    _, _, lanes = small_layout(unit_count, block_size)
    wide_at = scalar(lax.axis_index("wide"))
    pair_at = scalar(lax.axis_index("pair"))
    partner = [(p, p ^ 1) for p in range(pair_count)]
    across = [(p, p ^ 2) for p in range(pair_count)]

    block, small = pl.pallas_call(
        kernel_of(pack_kernel, unit_count),
        out_shape=(
            pltpu.VMEM((local_atoms, block_size, wide_row + lanes), BF16),
            pltpu.VMEM((local_atoms, block_size, lanes), BF16),
        ),
        in_specs=[SMEM, SMEM, SMEM, VMEM, VMEM, VMEM],
        out_specs=(VMEM, VMEM),
        name="pack",
    )(pair_at, occ_column.T, partner_live.T, three_center, occ_green, virt_green)
    two = small + lax.ppermute(small, "pair", partner)
    four = two + lax.ppermute(two, "pair", across)
    early = lax.dynamic_update_slice(block, two, (0, 0, wide_row))
    full = lax.dynamic_update_slice(block, four, (0, 0, wide_row))
    if wide_count == 8 and unit_count <= 2 * CHUNK:
        keep, send = respond_direct(early, full, two, wide_at, pair_at, unit_count, sizes)
    else:
        keep, send = respond_whole(full, pair_at, unit_count, sizes)
    return keep + lax.ppermute(send, "pair", partner)


def solution(mesh):
    placed = (
        P("wide", None, None),
        P("wide", "pair", None, None),
        P("wide", "pair", None, None),
        P("wide", "pair"),
        P("wide", "pair"),
    )
    return jax.shard_map(
        local, mesh=mesh, in_specs=placed, out_specs=P("pair", None), check_vma=False
    )
```
